128 devices in a mesh: gx: 16 (over y, z_lo, core), gy: 8 (over x, z_hi).
Axes of the slice: x: 4, y: 4, z: 4 (z_hi: 2, z_lo: 2; z = z_hi * 2 + z_lo), core: 2. Of those that a mesh axis runs over, the one named last changes fastest.
Arguments:
- thermal_anomaly_grid: float32 [30, 256, 2048], P(None, 'gy', 'gx'), may hold values from -5 to 5
- relative_moisture: float32 [30, 256, 2048], P(None, 'gy', 'gx'), may hold values from 0.05 to 1
- overcast_share: float32 [30, 256, 2048], P(None, 'gy', 'gx'), may hold values from 0 to 1
- sun_angle_projection: float32 [256, 2048], P('gy', 'gx'), may hold values from 0.1 to 1
- daylight_mask: int32 [16, 256], P('gx', 'gy'), may hold values 0 or 1
- radiator_owner_position: int32 [16, 256, 1], P('gx', 'gy'), may hold values from 0 to 15; in each aligned block of 32 rows (0 to 31, 32 to 63, ..., all dimensions but the last counted through in order) at most 4 rows name the same one
- molecular_opacity_lookup: bfloat16 [30, 140, 128], replicated, may hold values from 0.019897461 to 1.5
- condensed_opacity_per_share: float32 [140], replicated, may hold values from 0.05 to 1
- planck_emission_factor: float32 [140], replicated, may hold values from 0.2 to 1
- insolation_quadrature_factor: float32 [140], replicated, may hold values from 0.2 to 2
Outputs:
- advanced_anomaly_grid: float32 [30, 256, 2048], P(None, 'gy', 'gx')
- humidity_next: float32 [30, 256, 2048], P(None, 'gy', 'gx')
- ground_irradiance_slots: float32 [8, 16, 16, 4, 128], P('gy', 'gx')
The draws below stay inside these ranges and needn't reach their ends.
Inputs may be any that keep to these rules, and one draw needn't show every extreme that they name: `radiator_owner_position`: among the 32 blocks of one device, at most 4 name the same host, and some device's blocks name one host exactly 4 times.
All inputs are finite; a program needn't handle non-finite values. No bound on the sum of `daylight_mask` on one device may be relied on, other than what follows from the above.
Results may differ from the reference program's by a relative error of at most 0.0034.
Values may be sent and summed in bfloat16 or wider, within the bound.
A program may use at most 128 MiB of HBM per device.

```python
import math
import jax
import jax.numpy as jnp
import numpy as np
from jax import lax

STRATA_NUMBER = 30
G = 140
NT = 16
NQ = 8
CXT = 128
CYT = 32
NODES = 128
CAP = 4
EASTWARD_SPAN = 2048
NORTHWARD_SPAN = 256
N_GX = 16
N_GY = 8


def place_ends(result, own_key, low, high):
    dims = result.shape
    spot = [jax.random.randint(jax.random.fold_in(own_key, axis), (), 0, dims[axis]) for axis in range(len(dims))]
    result = result.at[tuple(spot)].set(low)
    longest = dims.index(max(dims))
    spot[longest] = (spot[longest] + 1) % dims[longest]
    return result.at[tuple(spot)].set(high)


def level_of(key, dims, pieces, low, largest):
    factor_of, own = 1.0, jax.random.fold_in(key, 6)
    for axis_at, parts in pieces:
        steps = jnp.exp(jax.random.uniform(jax.random.fold_in(own, axis_at), (parts,), jnp.float32, low / len(pieces), largest / len(pieces)))
        factor_of = factor_of * jnp.repeat(steps, dims[axis_at] // parts).reshape([-1 if axis == axis_at else 1 for axis in range(len(dims))])
    return factor_of


def shared_out(stream_key, own, number, rows, amount, top, most, skew):
    order = jax.random.permutation(stream_key, amount)
    packed, usual = load_shares(amount, rows * top, most, skew, True), load_shares(amount, rows * top, most, skew, False)
    places = jnp.arange(amount)

    def named(tallies, rotation):
        used = int((tallies > 0).sum())
        fixed = max(1, used // 4)
        moved = fixed + (places - fixed + rotation * (used - fixed)) % max(1, amount - fixed)
        return jnp.zeros((amount,), jnp.int32).at[order[jnp.where(places < fixed, places, moved)]].set(jnp.asarray(tallies, jnp.int32))

    tallies = jnp.where(number % 4 == 0, named(packed, number // 4), named(usual, number - number // 4 - 1))
    mixed = jax.random.permutation(jax.random.fold_in(own, 3), amount)
    donor, receiver = mixed[0:amount // 2 * 2:2], mixed[1:amount // 2 * 2:2]
    margin = jnp.minimum(tallies[donor] - 1, most - tallies[receiver]) // 2
    margin = jnp.where((donor == order[0]) | (receiver == order[0]) | (tallies[receiver] == 0), 0, jnp.maximum(margin, 0))
    moved = jax.random.randint(jax.random.fold_in(own, 4), (amount // 2,), 0, 1 << 20) % (margin + 1)
    tallies = tallies.at[donor].add(-moved).at[receiver].add(moved)
    members = jnp.searchsorted(jnp.cumsum(tallies), jnp.arange(rows * top), side="right").astype(jnp.int32)
    listing = members.reshape(top, rows).T
    listing = listing[jax.random.permutation(jax.random.fold_in(own, 1), rows)]
    rotation = jax.random.randint(jax.random.fold_in(own, 2), (rows, 1), 0, top)
    return jnp.take_along_axis(listing, (jnp.arange(top)[None, :] + rotation) % top, axis=1)


def load_shares(number_of, total, bound, lean, full):
    weights = [(1 << 20) // math.isqrt(grade ** lean) + 1 for grade in range(1, number_of + 1)]
    largest = bound if full else min(bound, max(-(-total // number_of), total * weights[0] // sum(weights)))
    least = 1 if total - largest >= number_of - 1 else 0
    holding, rest = [largest] + [least] * (number_of - 1), total - largest - least * (number_of - 1)
    while rest > 0:
        free = [i for i in range(1, number_of) if holding[i] < largest] or [i for i in range(1, number_of) if holding[i] < bound]
        whole, remaining = sum([weights[i] for i in free]), rest
        for i in free:
            more = min(bound - holding[i], max(1, remaining * weights[i] // whole), rest)
            holding[i] = holding[i] + more
            rest = rest - more
    return np.array(holding)


def bell_draw(stream_key, extent, deviation, most, pieces=(), held_as=jnp.bfloat16):
    values = jax.random.normal(stream_key, extent, jnp.float32) * deviation
    if len(pieces) > 0:
        values = level_of(stream_key, extent, pieces, -0.22, 0.18) * values
    return jnp.clip(values, min=-most, max=most).astype(held_as)


def setup_inputs(seed: int = 0) -> dict:
    arg_keys = jax.random.split(jax.random.key(seed), 11)
    thermal_anomaly_grid = bell_draw(arg_keys[0], (STRATA_NUMBER, NORTHWARD_SPAN, EASTWARD_SPAN), 1.0, 5.0, ((1, 8), (2, 16)), jnp.float32)
    relative_moisture = jnp.clip(0.05 + 0.95 * jax.random.uniform(arg_keys[1], (STRATA_NUMBER, NORTHWARD_SPAN, EASTWARD_SPAN), jnp.float32) ** level_of(arg_keys[1], (STRATA_NUMBER, NORTHWARD_SPAN, EASTWARD_SPAN), ((1, 8), (2, 16)), -0.2, 0.2), 0.05, 1.0)
    overcast_share = jnp.clip(1.0 * jax.random.uniform(arg_keys[2], (STRATA_NUMBER, NORTHWARD_SPAN, EASTWARD_SPAN), jnp.float32) ** level_of(arg_keys[2], (STRATA_NUMBER, NORTHWARD_SPAN, EASTWARD_SPAN), ((1, 8), (2, 16)), -0.2, 0.2), 0.0, 1.0)
    sun_angle_projection = jnp.clip(0.1 + 0.9 * jax.random.uniform(arg_keys[3], (NORTHWARD_SPAN, EASTWARD_SPAN), jnp.float32) ** level_of(arg_keys[3], (NORTHWARD_SPAN, EASTWARD_SPAN), ((0, 8), (1, 16)), -0.2, 0.2), 0.1, 1.0)
    daylight_mask = place_ends((jax.random.randint(arg_keys[4], (N_GX, NORTHWARD_SPAN), 0, 2) < 1).astype(jnp.int32), jax.random.fold_in(arg_keys[4], 1), 0, 1)
    radiator_owner_position_keys = jax.random.split(jax.random.fold_in(arg_keys[5], 1), N_GX * NORTHWARD_SPAN // CYT)
    radiator_owner_position_turns = jax.random.permutation(jax.random.fold_in(arg_keys[5], 3), N_GX * NORTHWARD_SPAN // CYT)
    radiator_owner_position = jax.vmap(lambda own, number: shared_out(jax.random.fold_in(arg_keys[5], 2), own, number, CYT, N_GX, 1, CAP, 2))(radiator_owner_position_keys, radiator_owner_position_turns).reshape((N_GX, NORTHWARD_SPAN, 1))
    molecular_opacity_lookup = jnp.clip(jnp.exp(jax.random.uniform(arg_keys[6], (STRATA_NUMBER, G, NODES), jnp.float32, math.log(0.019897461), math.log(1.5))), 0.019897461, 1.5).astype(jnp.bfloat16)
    condensed_opacity_per_share = jnp.clip(jnp.exp(jax.random.uniform(arg_keys[7], (G,), jnp.float32, math.log(0.05), math.log(1.0))), 0.05, 1.0)
    planck_emission_factor = jnp.clip(jnp.exp(jax.random.uniform(arg_keys[8], (G,), jnp.float32, math.log(0.2), math.log(1.0))), 0.2, 1.0)
    insolation_quadrature_factor = jnp.clip(jnp.exp(jax.random.uniform(arg_keys[9], (G,), jnp.float32, math.log(0.2), math.log(2.0))), 0.2, 2.0)
    return {"thermal_anomaly_grid": thermal_anomaly_grid, "relative_moisture": relative_moisture, "overcast_share": overcast_share, "sun_angle_projection": sun_angle_projection, "daylight_mask": daylight_mask, "radiator_owner_position": radiator_owner_position, "molecular_opacity_lookup": molecular_opacity_lookup, "condensed_opacity_per_share": condensed_opacity_per_share, "planck_emission_factor": planck_emission_factor, "insolation_quadrature_factor": insolation_quadrature_factor}


diffusion = 0.2
diffusivity = 1.66


def stencil(bordered_grid):
    centre = bordered_grid[:, :, 1:-1, 1:-1]
    beside_all = bordered_grid[:, :, 2:, 1:-1] + bordered_grid[:, :, :-2, 1:-1] + bordered_grid[:, :, 1:-1, 2:] + bordered_grid[:, :, 1:-1, :-2]
    return centre + diffusion * (beside_all - 4.0 * centre)


def optical_depth(layer, table_layer, condensed_opacity_per_share):
    air_temp, moisture, condensate = layer[0], layer[1], layer[2]
    temp_nodes = jnp.arange(NT, dtype=jnp.float32)
    humid_nodes = jnp.arange(NQ, dtype=jnp.float32)
    temp_pos = jnp.clip((air_temp + 3.0) * ((NT - 1.0) / 6.0), 0.0, NT - 1.0)
    humid_pos = jnp.clip(moisture * (NQ - 1.0), 0.0, NQ - 1.0)
    temp_hat = jnp.maximum(0.0, 1.0 - jnp.abs(temp_pos[None, :] - temp_nodes[:, None]))
    humid_hat = jnp.maximum(0.0, 1.0 - jnp.abs(humid_pos[None, :] - humid_nodes[:, None]))
    weights = (temp_hat[:, None, :] * humid_hat[None, :, :]).reshape(NT * NQ, -1).astype(jnp.bfloat16)
    gas_depth = jnp.dot(table_layer, weights, preferred_element_type=jnp.float32)
    return gas_depth + condensed_opacity_per_share[:, None] * condensate[None, :]


def column_physics(prognostic_bundle, zenith, incident, molecular_opacity_lookup, condensed_opacity_per_share, planck_emission_factor, insolation_quadrature_factor):
    layers = jnp.transpose(prognostic_bundle, (1, 0, 2))
    gpoints = planck_emission_factor.shape[0]

    def downward(carry, inputs):
        long_down, short_down = carry
        layer, table_layer = inputs
        depth = optical_depth(layer, table_layer, condensed_opacity_per_share)
        through = jnp.exp(-diffusivity * depth)
        source = planck_emission_factor[:, None] * (1.0 + 0.25 * layer[0][None, :])
        long_next = long_down * through + (1.0 - through) * source
        short_next = short_down * jnp.exp(-depth / zenith[None, :])
        gained = jnp.sum(long_down - long_next + short_down - short_next, axis=0)
        return (long_next, short_next), gained

    def upward(long_up, inputs):
        layer, table_layer = inputs
        depth = optical_depth(layer, table_layer, condensed_opacity_per_share)
        through = jnp.exp(-diffusivity * depth)
        source = planck_emission_factor[:, None] * (1.0 + 0.25 * layer[0][None, :])
        long_next = long_up * through + (1.0 - through) * source
        return long_next, jnp.sum(long_up - long_next, axis=0)

    start_long = jnp.zeros((gpoints, prognostic_bundle.shape[2]), jnp.float32)
    start_short = insolation_quadrature_factor[:, None] * incident[None, :]
    bottom, down_gain = lax.scan(downward, (start_long, start_short), (layers, molecular_opacity_lookup))
    start_up = planck_emission_factor[:, None] * (1.0 + 0.25 * layers[-1, 0][None, :])
    top_up, up_gain = lax.scan(upward, start_up, (layers, molecular_opacity_lookup), reverse=True)
    heating = (2.0 / gpoints) * (down_gain + up_gain)
    ground_irradiance_result = jnp.sum(bottom[0] + bottom[1], axis=0) / gpoints
    return heating, ground_irradiance_result


def reference(thermal_anomaly_grid, relative_moisture, overcast_share, sun_angle_projection, daylight_mask, radiator_owner_position, molecular_opacity_lookup, condensed_opacity_per_share, planck_emission_factor, insolation_quadrature_factor):
    gridded_quantities = jnp.stack((thermal_anomaly_grid, relative_moisture))
    laplacian_blurred_grid = stencil(jnp.pad(gridded_quantities, ((0, 0), (0, 0), (1, 1), (1, 1))))
    prognostic_bundle = jnp.stack((thermal_anomaly_grid, relative_moisture, overcast_share)).astype(jnp.bfloat16)
    prognostic_bundle = lax.optimization_barrier(prognostic_bundle).astype(jnp.float32)
    lit_columns = jnp.repeat(jnp.transpose(daylight_mask), CXT, axis=1).astype(jnp.float32)
    light = jnp.stack((sun_angle_projection, sun_angle_projection * lit_columns)).astype(jnp.bfloat16)
    light = lax.optimization_barrier(light).astype(jnp.float32)

    def one_row(row_index):
        start = row_index * CYT
        rows = lax.dynamic_slice_in_dim(prognostic_bundle, start, CYT, 2).reshape(3, STRATA_NUMBER, CYT * EASTWARD_SPAN)
        shine = lax.dynamic_slice_in_dim(light, start, CYT, 1).reshape(2, CYT * EASTWARD_SPAN)
        heating, ground_irradiance_result = column_physics(rows, shine[0], shine[1], molecular_opacity_lookup, condensed_opacity_per_share, planck_emission_factor, insolation_quadrature_factor)
        return heating.reshape(STRATA_NUMBER, CYT, EASTWARD_SPAN), ground_irradiance_result.reshape(CYT, EASTWARD_SPAN)

    heat_rows, surface_rows = lax.map(one_row, jnp.arange(N_GY, dtype=jnp.int32))
    warming_overall = jnp.transpose(heat_rows, (1, 0, 2, 3)).reshape(STRATA_NUMBER, NORTHWARD_SPAN, EASTWARD_SPAN)
    advanced_anomaly_grid = laplacian_blurred_grid[0] + warming_overall
    hosts = radiator_owner_position[:, :, 0].reshape(N_GX, N_GY, CYT)
    earlier = jnp.arange(CYT)[None, :] < jnp.arange(CYT)[:, None]
    same = hosts[:, :, :, None] == hosts[:, :, None, :]
    rank = jnp.sum(jnp.logical_and(same, earlier[None, None]), axis=3).astype(jnp.int32)
    host_ids = jnp.arange(N_GX, dtype=jnp.int32)[None, None, :, None, None]
    slot_ids = jnp.arange(CAP, dtype=jnp.int32)[None, None, None, :, None]
    pick = jnp.logical_and(hosts[:, :, None, None, :] == host_ids, rank[:, :, None, None, :] == slot_ids).astype(jnp.float32)
    profile_groups = surface_rows.reshape(N_GY, CYT, N_GX, CXT)
    ground_irradiance_slots = jnp.einsum("srhkb,rbsx->rhskx", pick, profile_groups, precision=lax.Precision.HIGHEST)
    return advanced_anomaly_grid, laplacian_blurred_grid[1], ground_irradiance_slots
```

```python
import jax
import jax.numpy as jnp
from jax import lax
from jax.experimental import pallas as pl
from jax.experimental.pallas import tpu as pltpu
from jax.sharding import PartitionSpec as P

CAP = 4
NHOST = 16
L=30; G=140; GP=144; NT=16; NQ=8; R=32; X=128; NC=9
LOG2E=1.4426950408889634
DIFF=1.66
f32=jnp.float32; bf16=jnp.bfloat16
W2=2*X

diffusion = 0.2

def extended(block, sides, width):
    for axis, dim in sides:
        count = lax.axis_size(axis)
        forward = [(i, i + 1) for i in range(count - 1)]
        backward = [(target, source) for source, target in forward]
        low = lax.ppermute(
            lax.slice_in_dim(block, block.shape[dim] - width, None, axis=dim), axis, forward
        )
        high = lax.ppermute(lax.slice_in_dim(block, 0, width, axis=dim), axis, backward)
        block = jnp.concatenate([low, block, high], axis=dim)
    return block


def stencil(bordered_grid):
    centre = bordered_grid[:, :, 1:-1, 1:-1]
    beside_all = (
        bordered_grid[:, :, 2:, 1:-1]
        + bordered_grid[:, :, :-2, 1:-1]
        + bordered_grid[:, :, 1:-1, 2:]
        + bordered_grid[:, :, 1:-1, :-2]
    )
    return centre + diffusion * (beside_all - 4.0 * centre)


def make(thpre=True, dotbf=False, pstore=True, pairs=16, kext=True, wbf=False, lev=1):
    KW=144 if kext else 128
    def kernel(t_ref,q_ref,c_ref,sun_ref,lit_ref,tab_ref,cond_ref,pl_ref,ins_ref, heat_ref,surf_ref,
               hp,cb,ss,ds,th,tabs,pg,qg,cg,tr,pd,zacc,bacc,hk):
        K=-DIFF*LOG2E
        ri=lax.broadcasted_iota(jnp.int32,(GP,G),0); ci=lax.broadcasted_iota(jnp.int32,(GP,G),1)
        eye=ri==ci
        def col(ref):
            return jnp.sum(jnp.where(eye,ref[...],0.0),axis=1,keepdims=True)
        pcol=col(pl_ref); qcol=col(ins_ref); ccol=col(cond_ref)*K
        psum=jnp.sum(pl_ref[...]); qsum=jnp.sum(ins_ref[...])
        pg[...]=jnp.broadcast_to(pcol,(GP,X)).astype(bf16)
        qg[...]=jnp.broadcast_to(qcol,(GP,X))
        lane=lax.broadcasted_iota(jnp.int32,(GP,16),1)
        chi=ccol.astype(bf16).astype(f32)
        cext=jnp.where(lane==0,chi,jnp.where(lane==1,ccol-chi,0.0)).astype(bf16)
        def prep(l,_):
            tabs[l,:,0:128]=jnp.concatenate([tab_ref[l].astype(f32)*K,jnp.zeros((GP-G,128),f32)],axis=0).astype(bf16)
            if kext: tabs[l,:,128:144]=cext
            t=t_ref[l].astype(bf16).astype(f32)
            tp=jnp.clip((t+3.0)*((NT-1.0)/6.0),0.0,NT-1.0)
            for i in range(NT):
                th[l,i]=jnp.maximum(0.0,1.0-jnp.abs(tp-float(i)))
            s=1.0+0.25*t
            ss[l]=s
            hp[l]=jnp.clip(q_ref[l].astype(bf16).astype(f32)*(NQ-1.0),0.0,NQ-1.0)
            cb[l]=c_ref[l].astype(bf16).astype(f32)
            return 0
        lax.fori_loop(0,L,prep,0)
        s=ss[...]
        ds[0:L-1]=s[:-1]-s[1:]
        i8=lax.broadcasted_iota(jnp.int32,(NQ,W2),0).astype(f32)
        ex=(lax.broadcasted_iota(jnp.int32,(16,W2),0)<2).astype(f32)
        lr=lax.broadcasted_iota(jnp.int32,(32,480),0); lc=lax.broadcasted_iota(jnp.int32,(32,480),1)>>4
        selz=jnp.where(lr==30,(lc==29).astype(f32),(lc==lr-1).astype(f32)-(lc==lr).astype(f32)).astype(bf16)
        selb=jnp.where(lr<30,(lc==lr+1).astype(f32)-(lc==lr).astype(f32),0.0).astype(bf16)
        def tree(v):
            ws=[v[16*i:16*i+16] for i in range(NC)]
            while len(ws)>1:
                ws=[a+b for a,b in zip(ws[0::2],ws[1::2])]+([ws[-1]] if len(ws)%2 else [])
            return ws[0]
        def pair(p,_):
            r0=2*p
            def row(ref,*l):
                return jnp.concatenate([ref[(*l,pl.ds(r0,1),slice(None))],ref[(*l,pl.ds(r0+1,1),slice(None))]],axis=1)
            sun=row(sun_ref)
            lit=jnp.concatenate([jnp.full((1,X),lit_ref[0,r0].astype(f32)),jnp.full((1,X),lit_ref[0,r0+1].astype(f32))],axis=1)
            mu=sun.astype(bf16).astype(f32)
            inv=((1.0/DIFF)/mu).astype(bf16)
            light=(sun*lit).astype(bf16).astype(f32)
            P=jnp.concatenate([pg[...],pg[...]],axis=1)
            E=-(P*row(ss,0).astype(bf16))
            S=(jnp.concatenate([qg[...],qg[...]],axis=1)*light).astype(bf16)
            def depth(l):
                hh=jnp.maximum(0.0,1.0-jnp.abs(row(hp,l)-i8))
                W=[row(th,l,i)*hh for i in range(NT)]
                W=[jnp.concatenate(W[2*i:2*i+2],axis=0).astype(bf16) for i in range(NT//2)]
                if kext: W.append((ex*row(cb,l)).astype(bf16))
                W=jnp.concatenate(W,axis=0)
                x=jnp.dot(tabs[l],W,preferred_element_type=bf16 if dotbf else f32)
                return x.astype(bf16)
            for l in range(L):
                x=depth(l)
                trl=jnp.exp2(x)
                tr[l]=trl
                ts=jnp.exp2(x*inv)
                Xl=trl*E
                S=S*ts
                zacc[16*l:16*l+16]=tree(Xl+S)
                if l<L-1:
                    pds=P*row(ds,l).astype(bf16)
                    if pstore: pd[l]=pds
                    E=Xl+pds
            F=jnp.zeros((GP,W2),bf16)
            for l in range(L-1,-1,-1):
                Y=tr[l]*F if l<L-1 else F
                bacc[16*l:16*l+16]=tree(Y) if l<L-1 else jnp.zeros((16,W2),bf16)
                if l>0:
                    pds=pd[l-1] if pstore else P*row(ds,l-1).astype(bf16)
                    F=Y-pds
            h=jnp.dot(selz,zacc[...],preferred_element_type=f32)+jnp.dot(selb,bacc[...],preferred_element_type=f32)
            for k in range(2):
                hk[pl.ds(r0+k,32,stride=32),:]=h[:,X*k:X*k+X]
            return 0
        lax.fori_loop(0,pairs,pair,0)
        for l in range(L):
            g=hk[32*l:32*l+32]
            if l==0: g=g-psum*ss[0]
            else: g=g+psum*ds[l-1]
            if l<L-1: g=g-psum*ds[l]
            heat_ref[l]=g*(2.0/G)
        def lrow(r,_):
            li=(sun_ref[pl.ds(r,1),:]*lit_ref[0,r].astype(f32)).astype(bf16).astype(f32)
            heat_ref[0,pl.ds(r,1),:]=heat_ref[0,pl.ds(r,1),:]+qsum*(2.0/G)*li
            return 0
        lax.fori_loop(0,R,lrow,0)
        surf_ref[...]=(hk[32*30:32*31]+psum*ss[L-1])*(1.0/G)
    def run(t,q,c,sun,lit,table,cond,planck,insol):
        V=pltpu.VMEM
        fld=V((L,R,X),f32)
        vm=pl.BlockSpec(memory_space=pltpu.VMEM)
        return pl.pallas_call(kernel,out_shape=(jax.ShapeDtypeStruct((L,R,X),f32),jax.ShapeDtypeStruct((R,X),f32)),
            in_specs=[vm]*4+[pl.BlockSpec(memory_space=pltpu.SMEM)]+[vm]*4,
            scratch_shapes=[fld,fld,fld,fld,V((L,NT,R,X),f32),V((L,GP,KW),bf16),V((GP,X),bf16),V((GP,X),f32),V((GP,X),f32),
              V((L,GP,W2),bf16),V((L,GP,W2),bf16),V((480,W2),bf16),V((480,W2),bf16),V((1024,X),f32)],
            compiler_params=pltpu.CompilerParams(vmem_limit_bytes=56*2**20),
            )(t,q,c,sun,lit.reshape(1,R),table,cond.reshape(1,G),planck.reshape(1,G),insol.reshape(1,G))
    return run


def on_device(t, q, c, sun, lit, owner, table, cond, planck, insol):
    bordered = extended(jnp.stack((t, q)), (("gx", 3), ("gy", 2)), 1)
    blurred = stencil(bordered)
    heat, surf = make()(t, q, c, sun, lit[0], table, cond, planck, insol)
    own = owner[0, :, 0]
    earlier = jnp.arange(R)[None, :] < jnp.arange(R)[:, None]
    rank = jnp.sum(jnp.logical_and(own[:, None] == own[None, :], earlier), axis=1)
    place = own * CAP + rank
    pick = (place[None, :] == jnp.arange(NHOST * CAP)[:, None]).astype(f32)
    slots = jnp.dot(pick, surf, precision=lax.Precision.HIGHEST).reshape(NHOST, CAP, X)
    got = lax.all_to_all(slots, "gx", split_axis=0, concat_axis=0, tiled=True)
    return blurred[0] + heat, blurred[1], got[None, None]

def solution(mesh):
    placed = (
        P(None, "gy", "gx"),
        P(None, "gy", "gx"),
        P(None, "gy", "gx"),
        P("gy", "gx"),
        P("gx", "gy"),
        P("gx", "gy", None),
        P(),
        P(),
        P(),
        P(),
    )
    return jax.shard_map(
        on_device,
        mesh=mesh,
        in_specs=placed,
        out_specs=(P(None, "gy", "gx"), P(None, "gy", "gx"), P("gy", "gx", None, None, None)),
        check_vma=False,
    )
```

```python
import jax
import jax.numpy as jnp
from jax import lax
from jax.experimental import pallas as pl
from jax.experimental.pallas import tpu as pltpu
from jax.sharding import PartitionSpec as P

L, G, GP, NT, NQ, R, X = 30, 140, 144, 16, 8, 32, 128
NC = GP // 16
KW = 144
W2 = 2 * X
PAIRS = R // 2
CAP = 4
N_GX, N_GY = 16, 8
CH = 5
NK = L // CH
diffusion = 0.2
diffusivity = 1.66
SCALE = -diffusivity * 1.4426950408889634
f32, bf16 = jnp.float32, jnp.bfloat16


def kernel(
    t_ref, q_ref, c_ref, sun_ref, lit_ref, own_ref, tab_ref, cond_ref, planck_ref, insol_ref,
    adv_ref, hum_ref, slot_ref,
    hp, cb, ss, ds, th, tabs, pg, qg, tr_a, tr_b, pd_a, pd_b, zacc, bacc, hk, hz, inc, sf,
    xb, Es, Ss, Fs, iv, nsend, nrecv, esend, erecv, ssend, srecv,
    halo_out, halo_in, slot_out, slot_in,
):
    gx, gy = lax.axis_index("gx"), lax.axis_index("gy")
    barrier = pltpu.get_barrier_semaphore()
    mates = [{"gx": lax.rem(gx + d, N_GX), "gy": gy} for d in range(1, N_GX)]
    beside = [{"gx": gx, "gy": lax.rem(gy + d, N_GY)} for d in (1, N_GY - 1)]
    for one_device in mates + beside:
        pl.semaphore_signal(barrier, inc=1, device_id=one_device, device_id_type=pl.DeviceIdType.MESH)

    trs, pds = (tr_a, tr_b), (pd_a, pd_b)

    eye = lax.broadcasted_iota(jnp.int32, (GP, G), 0) == lax.broadcasted_iota(jnp.int32, (GP, G), 1)

    def column(ref):
        return jnp.sum(jnp.where(eye, ref[...], 0.0), axis=1, keepdims=True)

    ccol = column(cond_ref) * SCALE
    psum, qsum = jnp.sum(planck_ref[...]), jnp.sum(insol_ref[...])
    pg[...] = jnp.broadcast_to(column(planck_ref), (GP, X)).astype(bf16)
    qg[...] = jnp.broadcast_to(column(insol_ref), (GP, X))
    lane16 = lax.broadcasted_iota(jnp.int32, (GP, 16), 1)
    chi = ccol.astype(bf16).astype(f32)
    cext = jnp.where(lane16 == 0, chi, jnp.where(lane16 == 1, ccol - chi, 0.0)).astype(bf16)
    lane = lax.broadcasted_iota(jnp.int32, (R, X), 1)
    line = lax.broadcasted_iota(jnp.int32, (R, X), 0)
    nsend[...] = jnp.zeros_like(nsend)
    ds[0] = jnp.zeros((R, X), f32)

    def prepare(l, edges):
        tabs[l, :, 0:NT * NQ] = jnp.concatenate(
            [tab_ref[l].astype(f32) * SCALE, jnp.zeros((GP - G, NT * NQ), f32)], axis=0
        ).astype(bf16)
        tabs[l, :, NT * NQ:KW] = cext
        warm, wet = t_ref[l], q_ref[l]
        t = warm.astype(bf16).astype(f32)
        tp = jnp.clip((t + 3.0) * ((NT - 1.0) / 6.0), 0.0, NT - 1.0)
        for i in range(NT):
            th[l, i] = jnp.maximum(0.0, 1.0 - jnp.abs(tp - float(i)))
        s = 1.0 + 0.25 * t
        ss[l] = s
        ds[l] = edges[4] - s
        hp[l] = jnp.clip(wet.astype(bf16).astype(f32) * (NQ - 1.0), 0.0, NQ - 1.0)
        cb[l] = c_ref[l].astype(bf16).astype(f32)
        here = lane == l
        out = []
        for field, v in enumerate((warm, wet)):
            nsend[0, field, pl.ds(l, 1), :] = v[0:1]
            nsend[1, field, pl.ds(l, 1), :] = v[R - 1:R]
            out.append(jnp.where(here, pltpu.roll(v, l, 1), edges[2 * field]))
            out.append(jnp.where(here, pltpu.roll(v, l + 1, 1), edges[2 * field + 1]))
        return tuple(out) + (s,)

    none = jnp.zeros((R, X), f32)
    edges = lax.fori_loop(0, L, prepare, (none,) * 5)
    ds[L] = none
    for field in range(2):
        for side in range(2):
            esend[side, field] = edges[2 * field + side]

    pl.semaphore_wait(barrier, N_GX + 1)
    west, east = {"gx": lax.rem(gx + N_GX - 1, N_GX), "gy": gy}, {"gx": lax.rem(gx + 1, N_GX), "gy": gy}
    south, north = {"gx": gx, "gy": lax.rem(gy + N_GY - 1, N_GY)}, {"gx": gx, "gy": lax.rem(gy + 1, N_GY)}
    halos = []
    for n, (src, dst, target) in enumerate((
        (esend.at[0], erecv.at[1], west), (esend.at[1], erecv.at[0], east),
        (nsend.at[0], nrecv.at[1], south), (nsend.at[1], nrecv.at[0], north),
    )):
        halos.append(pltpu.make_async_remote_copy(
            src_ref=src, dst_ref=dst, send_sem=halo_out.at[n], recv_sem=halo_in.at[n],
            device_id=target, device_id_type=pl.DeviceIdType.MESH,
        ))
        halos[-1].start()

    i8 = lax.broadcasted_iota(jnp.int32, (NQ, W2), 0).astype(f32)
    ex = (lax.broadcasted_iota(jnp.int32, (16, W2), 0) < 2).astype(f32)
    lr = lax.broadcasted_iota(jnp.int32, (32, 16 * L), 0)
    lc = lax.broadcasted_iota(jnp.int32, (32, 16 * L), 1) >> 4
    selz = jnp.where(
        lr == L, (lc == L - 1).astype(f32), (lc == lr - 1).astype(f32) - (lc == lr).astype(f32)
    ).astype(bf16)
    selb = jnp.where(lr < L, (lc == lr + 1).astype(f32) - (lc == lr).astype(f32), 0.0).astype(bf16)

    def tree(v):
        parts = [v[16 * i:16 * i + 16] for i in range(NC)]
        while len(parts) > 1:
            parts = [a + b for a, b in zip(parts[0::2], parts[1::2])] + (
                [parts[-1]] if len(parts) % 2 else []
            )
        return parts[0]

    def row(ref, r0, *at):
        return jnp.concatenate(
            [ref[(*at, pl.ds(r0, 1), slice(None))], ref[(*at, pl.ds(r0 + 1, 1), slice(None))]], axis=1
        )

    def both(v):
        return jnp.concatenate([v, v], axis=1)

    def depth(p, l, j):
        r0 = 2 * p
        hh = jnp.maximum(0.0, 1.0 - jnp.abs(row(hp, r0, l) - i8))
        w = [row(th, r0, l, i) * hh for i in range(NT)]
        w = [jnp.concatenate(w[2 * i:2 * i + 2], axis=0).astype(bf16) for i in range(NT // 2)]
        w.append((ex * row(cb, r0, l)).astype(bf16))
        xb[j] = jnp.dot(
            tabs[l], jnp.concatenate(w, axis=0), preferred_element_type=f32
        ).astype(bf16)

    def start(p):
        r0 = 2 * p
        sun = row(sun_ref, r0)
        lit = jnp.concatenate(
            [jnp.full((1, X), lit_ref[0, r0 + k].astype(f32)) for k in range(2)], axis=1
        )
        iv[...] = jnp.broadcast_to(
            (1.0 / diffusivity) / sun.astype(bf16).astype(f32), (16, W2)
        ).astype(bf16)
        light = (sun * lit).astype(bf16).astype(f32)
        for k in range(2):
            inc[pl.ds(r0 + k, 1), :] = light[:, X * k:X * k + X]
        Es[...] = both(pg[...]) * row(ds, r0, 0).astype(bf16)
        Ss[...] = (both(qg[...]) * light).astype(bf16)

    def down(p, k, par):
        r0 = 2 * p
        E, S = Es[...], Ss[...]
        inv = jnp.concatenate([iv[...]] * NC, axis=0)
        for j in range(CH):
            l = k * CH + j
            x = xb[j]
            trl = jnp.exp2(x)
            trs[par][l] = trl
            down_part = trl * E
            S = S * jnp.exp2(x * inv)
            zacc[l] = tree(down_part + S)
            step = both(pg[...]) * row(ds, r0, l + 1).astype(bf16)
            pds[par][l + 1] = step
            E = down_part + step
        Es[...] = E
        Ss[...] = S

    def up(k, par):
        F = Fs[...]
        for j in range(CH):
            l = L - 1 - (k * CH + j)
            up_part = trs[par][l] * F
            bacc[l] = tree(up_part)
            F = up_part - pds[par][l]
        Fs[...] = F

    def down_sums(p):
        h = jnp.dot(selz, zacc[...].reshape(16 * L, W2), preferred_element_type=f32)
        hz[...] = h
        for k in range(2):
            sf[pl.ds(2 * p + k, 1), :] = h[L:L + 1, X * k:X * k + X]

    def up_sums(p):
        h = hz[...] + jnp.dot(selb, bacc[...].reshape(16 * L, W2), preferred_element_type=f32)
        for k in range(2):
            hk[pl.ds(2 * p + k, 32, stride=32), :] = h[:, X * k:X * k + X]

    def chunks(body):
        def step(k, carry):
            body(k)
            return carry

        lax.fori_loop(0, NK, step, 0)

    def next_and_down(p, k, par):
        n = p * NK + k + 1
        pn, kn = lax.rem(lax.div(n, NK), PAIRS), lax.rem(n, NK)
        down(p, k, par)
        for j in range(CH):
            depth(pn, kn * CH + j, j)

    def whole(p, par):
        start(p)
        Fs[...] = jnp.zeros((GP, W2), bf16)

        def body(k):
            up(k, 1 - par)
            next_and_down(p, k, par)

        chunks(body)
        up_sums(p - 1)
        down_sums(p)

    for ref in pds:
        ref[0] = jnp.zeros((GP, W2), bf16)
    for j in range(CH):
        depth(0, j, j)
    start(0)
    chunks(lambda k: next_and_down(0, k, 0))
    down_sums(0)

    def two(i, carry):
        whole(2 * i + 1, 1)
        whole(2 * i + 2, 0)
        return carry

    lax.fori_loop(0, (PAIRS - 2) // 2, two, 0)
    whole(PAIRS - 1, 1)

    surface = (sf[...] + psum * ss[L - 1]) * (1.0 / G)
    own = own_ref[...].reshape(R, 1).astype(f32)
    er = lax.broadcasted_iota(jnp.int32, (R, R), 0)
    ec = lax.broadcasted_iota(jnp.int32, (R, R), 1)
    own_row = jnp.sum(jnp.where(er == ec, own, 0.0), axis=0, keepdims=True)
    rank = jnp.sum(
        jnp.where(jnp.logical_and(er < ec, own == own_row), 1.0, 0.0), axis=0, keepdims=True
    )
    pick = lax.broadcasted_iota(jnp.int32, (8 * N_GX, R), 0).astype(f32) == own_row * 8.0 + rank
    slots = jnp.dot(
        pick.astype(f32), surface, precision=lax.Precision.HIGHEST, preferred_element_type=f32
    )
    ssend[...] = slots.reshape(N_GX, 8, X)
    sends = []
    for d in range(1, N_GX):
        to = lax.rem(gx + d, N_GX)
        sends.append(pltpu.make_async_remote_copy(
            src_ref=ssend.at[to], dst_ref=srecv.at[gx], send_sem=slot_out.at[d],
            recv_sem=slot_in.at[d], device_id={"gx": to, "gy": gy},
            device_id_type=pl.DeviceIdType.MESH,
        ))
        sends[-1].start()

    Fs[...] = jnp.zeros((GP, W2), bf16)
    chunks(lambda k: up(k, 1))
    up_sums(PAIRS - 1)

    hk[0:R] = hk[0:R] + qsum * inc[...]
    for copy in halos:
        copy.wait()
    inside_w = (gx > 0).astype(f32)
    inside_e = (gx < N_GX - 1).astype(f32)
    inside_s = (gy > 0).astype(f32)
    inside_n = (gy < N_GY - 1).astype(f32)

    def smooth(l, field, v):
        low = jnp.where(line == 0, nrecv[0, field, pl.ds(l, 1), :] * inside_s, pltpu.roll(v, 1, 0))
        high = jnp.where(
            line == R - 1, nrecv[1, field, pl.ds(l, 1), :] * inside_n, pltpu.roll(v, R - 1, 0)
        )
        left = jnp.where(
            lane == 0, pltpu.roll(erecv[0, field], lax.rem(X - l, X), 1) * inside_w, pltpu.roll(v, 1, 1)
        )
        right = jnp.where(
            lane == X - 1, pltpu.roll(erecv[1, field], X - 1 - l, 1) * inside_e,
            pltpu.roll(v, X - 1, 1),
        )
        return v + diffusion * (low + high + left + right - 4.0 * v)

    def last(l, carry):
        gain = hk[pl.ds(pl.multiple_of(R * l, R), R), :] + psum * (ds[l] - ds[l + 1])
        adv_ref[l] = smooth(l, 0, t_ref[l]) + gain * (2.0 / G)
        hum_ref[l] = smooth(l, 1, q_ref[l])
        return carry

    lax.fori_loop(0, L, last, 0)
    for copy in sends:
        copy.wait()
    srecv[gx] = ssend[gx]
    slot_ref[...] = srecv[:, 0:CAP, :]


def on_device(t, q, c, sun, lit, owner, table, cond, planck, insol):
    vmem, scratch = pl.BlockSpec(memory_space=pltpu.VMEM), pltpu.VMEM
    field = scratch((L, R, X), f32)
    levels = scratch((L, GP, W2), bf16)
    state = scratch((GP, W2), bf16)
    out = pl.pallas_call(
        kernel,
        out_shape=(
            jax.ShapeDtypeStruct((L, R, X), f32),
            jax.ShapeDtypeStruct((L, R, X), f32),
            jax.ShapeDtypeStruct((N_GX, CAP, X), f32),
        ),
        in_specs=[vmem] * 4 + [pl.BlockSpec(memory_space=pltpu.SMEM)] + [vmem] * 5,
        out_specs=(vmem,) * 3,
        scratch_shapes=[
            field, field, field, scratch((L + 1, R, X), f32), scratch((L, NT, R, X), f32),
            scratch((L, GP, KW), bf16), scratch((GP, X), bf16), scratch((GP, X), f32),
            levels, levels, scratch((L + 1, GP, W2), bf16), scratch((L + 1, GP, W2), bf16),
            scratch((L, 16, W2), bf16), scratch((L, 16, W2), bf16),
            scratch((32 * R, X), f32), scratch((32, W2), f32), scratch((R, X), f32),
            scratch((R, X), f32), scratch((CH, GP, W2), bf16), state, state, state,
            scratch((16, W2), bf16),
            scratch((2, 2, R, X), f32), scratch((2, 2, R, X), f32),
            scratch((2, 2, R, X), f32), scratch((2, 2, R, X), f32),
            scratch((N_GX, 8, X), f32), scratch((N_GX, 8, X), f32),
            pltpu.SemaphoreType.DMA((4,)), pltpu.SemaphoreType.DMA((4,)),
            pltpu.SemaphoreType.DMA((N_GX,)), pltpu.SemaphoreType.DMA((N_GX,)),
        ],
        compiler_params=pltpu.CompilerParams(
            collective_id=0, has_side_effects=True, vmem_limit_bytes=56 * 2**20
        ),
    )(t, q, c, sun, lit, owner, table, cond[None], planck[None], insol[None])
    return out[0], out[1], out[2][None, None]


def solution(mesh):
    placed = (
        P(None, "gy", "gx"),
        P(None, "gy", "gx"),
        P(None, "gy", "gx"),
        P("gy", "gx"),
        P("gx", "gy"),
        P("gx", "gy", None),
        P(),
        P(),
        P(),
        P(),
    )
    return jax.shard_map(
        on_device,
        mesh=mesh,
        in_specs=placed,
        out_specs=(P(None, "gy", "gx"), P(None, "gy", "gx"), P("gy", "gx", None, None, None)),
        check_vma=False,
    )
```

```python
import jax
import jax.numpy as jnp
from jax import lax
from jax.experimental import pallas as pl
from jax.experimental.pallas import tpu as pltpu
from jax.sharding import PartitionSpec as P

L, G, GP, NT, NQ, R, X = 30, 140, 144, 16, 8, 32, 128
NC = GP // 16
KW = 144
W2 = 2 * X
PAIRS = R // 2
CAP = 4
N_GX, N_GY = 16, 8
CH = 10
NK = L // CH
diffusion = 0.2
diffusivity = 1.66
SCALE = -diffusivity * 1.4426950408889634
f32, bf16 = jnp.float32, jnp.bfloat16


def kernel(
    t_ref, q_ref, c_ref, sun_ref, lit_ref, place_ref, tab_ref, cond_ref, planck_ref, insol_ref,
    gain_ref, halo_ref, slot_ref,
    hp, cb, ss, ds, th, tabs, pg, qg, tr_a, tr_b, pd_a, pd_b, zacc, bacc, hk, hz, inc, sf,
    xb, Es, Ss, Fs, iv, nsend, nrecv, esend, erecv, ssend, srecv,
    halo_out, halo_in, slot_out, slot_in,
):
    gx, gy = lax.axis_index("gx"), lax.axis_index("gy")
    barrier = pltpu.get_barrier_semaphore()
    mates = [{"gx": lax.rem(gx + d, N_GX), "gy": gy} for d in range(1, N_GX)]
    beside = [{"gx": gx, "gy": lax.rem(gy + d, N_GY)} for d in (1, N_GY - 1)]
    for one_device in mates + beside:
        pl.semaphore_signal(barrier, inc=1, device_id=one_device, device_id_type=pl.DeviceIdType.MESH)

    trs, pds = (tr_a, tr_b), (pd_a, pd_b)

    eye = lax.broadcasted_iota(jnp.int32, (GP, G), 0) == lax.broadcasted_iota(jnp.int32, (GP, G), 1)

    def column(ref):
        return jnp.sum(jnp.where(eye, ref[...], 0.0), axis=1, keepdims=True)

    ccol = column(cond_ref) * SCALE
    psum, qsum = jnp.sum(planck_ref[...]), jnp.sum(insol_ref[...])
    pg[...] = jnp.broadcast_to(column(planck_ref), (GP, X)).astype(bf16)
    qg[...] = jnp.broadcast_to(column(insol_ref), (GP, X))
    lane16 = lax.broadcasted_iota(jnp.int32, (GP, 16), 1)
    chi = ccol.astype(bf16).astype(f32)
    cext = jnp.where(lane16 == 0, chi, jnp.where(lane16 == 1, ccol - chi, 0.0)).astype(bf16)
    lane = lax.broadcasted_iota(jnp.int32, (R, X), 1)
    nsend[...] = jnp.zeros_like(nsend)
    ds[0] = jnp.zeros((R, X), f32)

    def prepare(l, edges):
        tabs[l, :, 0:NT * NQ] = jnp.concatenate(
            [tab_ref[l].astype(f32) * SCALE, jnp.zeros((GP - G, NT * NQ), f32)], axis=0
        ).astype(bf16)
        tabs[l, :, NT * NQ:KW] = cext
        warm, wet = t_ref[l], q_ref[l]
        t = warm.astype(bf16).astype(f32)
        tp = jnp.clip((t + 3.0) * ((NT - 1.0) / 6.0), 0.0, NT - 1.0)
        for i in range(NT):
            th[l, i] = jnp.maximum(0.0, 1.0 - jnp.abs(tp - float(i)))
        s = 1.0 + 0.25 * t
        ss[l] = s
        ds[l] = edges[4] - s
        hp[l] = jnp.clip(wet.astype(bf16).astype(f32) * (NQ - 1.0), 0.0, NQ - 1.0)
        cb[l] = c_ref[l].astype(bf16).astype(f32)
        here = lane == l
        out = []
        for field, v in enumerate((warm, wet)):
            nsend[0, field, pl.ds(l, 1), :] = v[0:1]
            nsend[1, field, pl.ds(l, 1), :] = v[R - 1:R]
            out.append(jnp.where(here, pltpu.roll(v, l, 1), edges[2 * field]))
            out.append(jnp.where(here, pltpu.roll(v, l + 1, 1), edges[2 * field + 1]))
        return tuple(out) + (s,)

    none = jnp.zeros((R, X), f32)
    edges = lax.fori_loop(0, L, prepare, (none,) * 5)
    ds[L] = none
    for field in range(2):
        for side in range(2):
            esend[side, field] = edges[2 * field + side]

    pl.semaphore_wait(barrier, N_GX + 1)
    west, east = {"gx": lax.rem(gx + N_GX - 1, N_GX), "gy": gy}, {"gx": lax.rem(gx + 1, N_GX), "gy": gy}
    south, north = {"gx": gx, "gy": lax.rem(gy + N_GY - 1, N_GY)}, {"gx": gx, "gy": lax.rem(gy + 1, N_GY)}
    halos = []
    for n, (src, dst, target) in enumerate((
        (esend.at[0], erecv.at[1], west), (esend.at[1], erecv.at[0], east),
        (nsend.at[0], nrecv.at[1], south), (nsend.at[1], nrecv.at[0], north),
    )):
        halos.append(pltpu.make_async_remote_copy(
            src_ref=src, dst_ref=dst, send_sem=halo_out.at[n], recv_sem=halo_in.at[n],
            device_id=target, device_id_type=pl.DeviceIdType.MESH,
        ))
        halos[-1].start()

    i8 = lax.broadcasted_iota(jnp.int32, (NQ, W2), 0).astype(f32)
    ex = (lax.broadcasted_iota(jnp.int32, (16, W2), 0) < 2).astype(f32)
    lr = lax.broadcasted_iota(jnp.int32, (32, 16 * L), 0)
    lc = lax.broadcasted_iota(jnp.int32, (32, 16 * L), 1) >> 4
    selz = jnp.where(
        lr == L, (lc == L - 1).astype(f32), (lc == lr - 1).astype(f32) - (lc == lr).astype(f32)
    ).astype(bf16)
    selb = jnp.where(lr < L, (lc == lr + 1).astype(f32) - (lc == lr).astype(f32), 0.0).astype(bf16)

    def tree(v):
        parts = [v[16 * i:16 * i + 16] for i in range(NC)]
        while len(parts) > 1:
            parts = [a + b for a, b in zip(parts[0::2], parts[1::2])] + (
                [parts[-1]] if len(parts) % 2 else []
            )
        return parts[0]

    def row(ref, r0, *at):
        return jnp.concatenate(
            [ref[(*at, pl.ds(r0, 1), slice(None))], ref[(*at, pl.ds(r0 + 1, 1), slice(None))]], axis=1
        )

    def both(v):
        return jnp.concatenate([v, v], axis=1)

    def depth(p, l, j):
        r0 = 2 * p
        hh = jnp.maximum(0.0, 1.0 - jnp.abs(row(hp, r0, l) - i8))
        w = [row(th, r0, l, i) * hh for i in range(NT)]
        w = [jnp.concatenate(w[2 * i:2 * i + 2], axis=0).astype(bf16) for i in range(NT // 2)]
        w.append((ex * row(cb, r0, l)).astype(bf16))
        xb[j] = jnp.dot(
            tabs[l], jnp.concatenate(w, axis=0), preferred_element_type=f32
        ).astype(bf16)

    def start(p):
        r0 = 2 * p
        sun = row(sun_ref, r0)
        lit = jnp.concatenate(
            [jnp.full((1, X), lit_ref[0, r0 + k].astype(f32)) for k in range(2)], axis=1
        )
        iv[...] = jnp.broadcast_to(
            (1.0 / diffusivity) / sun.astype(bf16).astype(f32), (16, W2)
        ).astype(bf16)
        light = (sun * lit).astype(bf16).astype(f32)
        for k in range(2):
            inc[pl.ds(r0 + k, 1), :] = light[:, X * k:X * k + X]
        Es[...] = both(pg[...]) * row(ds, r0, 0).astype(bf16)
        Ss[...] = (both(qg[...]) * light).astype(bf16)

    def down(p, k, par):
        r0 = 2 * p
        E, S = Es[...], Ss[...]
        inv = jnp.concatenate([iv[...]] * NC, axis=0)
        for j in range(CH):
            l = k * CH + j
            x = xb[j]
            trl = jnp.exp2(x)
            trs[par][l] = trl
            down_part = trl * E
            S = S * jnp.exp2(x * inv)
            zacc[l] = tree(down_part + S)
            step = both(pg[...]) * row(ds, r0, l + 1).astype(bf16)
            pds[par][l + 1] = step
            E = down_part + step
        Es[...] = E
        Ss[...] = S

    def up(k, par):
        F = Fs[...]
        for j in range(CH):
            l = L - 1 - (k * CH + j)
            up_part = trs[par][l] * F
            bacc[l] = tree(up_part)
            F = up_part - pds[par][l]
        Fs[...] = F

    def down_sums(p):
        h = jnp.dot(selz, zacc[...].reshape(16 * L, W2), preferred_element_type=f32)
        hz[...] = h
        for k in range(2):
            sf[pl.ds(2 * p + k, 1), :] = h[L:L + 1, X * k:X * k + X]

    def up_sums(p):
        h = hz[...] + jnp.dot(selb, bacc[...].reshape(16 * L, W2), preferred_element_type=f32)
        for k in range(2):
            hk[pl.ds(2 * p + k, 32, stride=32), :] = h[:, X * k:X * k + X]

    def chunks(body):
        def step(k, carry):
            body(k)
            return carry

        lax.fori_loop(0, NK, step, 0)

    def next_and_down(p, k, par):
        n = p * NK + k + 1
        pn, kn = lax.rem(lax.div(n, NK), PAIRS), lax.rem(n, NK)
        down(p, k, par)
        for j in range(CH):
            depth(pn, kn * CH + j, j)

    def whole(p, par):
        start(p)
        Fs[...] = jnp.zeros((GP, W2), bf16)

        def body(k):
            up(k, 1 - par)
            next_and_down(p, k, par)

        chunks(body)
        up_sums(p - 1)
        down_sums(p)

    for ref in pds:
        ref[0] = jnp.zeros((GP, W2), bf16)
    for j in range(CH):
        depth(0, j, j)
    start(0)
    chunks(lambda k: next_and_down(0, k, 0))
    down_sums(0)

    def two(i, carry):
        whole(2 * i + 1, 1)
        whole(2 * i + 2, 0)
        return carry

    lax.fori_loop(0, (PAIRS - 2) // 2, two, 0)
    whole(PAIRS - 1, 1)

    surface = (sf[...] + psum * ss[L - 1]) * (1.0 / G)
    pick = lax.broadcasted_iota(jnp.int32, (8 * N_GX, R), 0).astype(f32) == place_ref[...]
    slots = jnp.dot(
        pick.astype(f32), surface, precision=lax.Precision.HIGHEST, preferred_element_type=f32
    )
    ssend[...] = slots.reshape(N_GX, 8, X)
    sends = []
    for d in range(1, N_GX):
        to = lax.rem(gx + d, N_GX)
        sends.append(pltpu.make_async_remote_copy(
            src_ref=ssend.at[to], dst_ref=srecv.at[gx], send_sem=slot_out.at[d],
            recv_sem=slot_in.at[d], device_id={"gx": to, "gy": gy},
            device_id_type=pl.DeviceIdType.MESH,
        ))
        sends[-1].start()

    Fs[...] = jnp.zeros((GP, W2), bf16)
    chunks(lambda k: up(k, 1))
    up_sums(PAIRS - 1)

    hk[0:R] = hk[0:R] + qsum * inc[...]
    for l in range(L):
        gain_ref[l] = (hk[R * l:R * l + R] + psum * (ds[l] - ds[l + 1])) * (2.0 / G)
    for copy in halos:
        copy.wait()
    halo_ref[0] = erecv[0] * (gx > 0).astype(f32)
    halo_ref[1] = erecv[1] * (gx < N_GX - 1).astype(f32)
    halo_ref[2] = nrecv[0] * (gy > 0).astype(f32)
    halo_ref[3] = nrecv[1] * (gy < N_GY - 1).astype(f32)
    for copy in sends:
        copy.wait()
    srecv[gx] = ssend[gx]
    slot_ref[...] = srecv[...]


def finish(t_ref, q_ref, gain_ref, halo_ref, slot_ref, adv_ref, hum_ref, out_ref):
    lane = lax.broadcasted_iota(jnp.int32, (R, X), 1)
    line = lax.broadcasted_iota(jnp.int32, (R, X), 0)

    def smooth(l, field, v):
        low = jnp.where(line == 0, halo_ref[2, field, l:l + 1, :], pltpu.roll(v, 1, 0))
        high = jnp.where(line == R - 1, halo_ref[3, field, l:l + 1, :], pltpu.roll(v, R - 1, 0))
        left = jnp.where(
            lane == 0, pltpu.roll(halo_ref[0, field], (X - l) % X, 1), pltpu.roll(v, 1, 1)
        )
        right = jnp.where(
            lane == X - 1, pltpu.roll(halo_ref[1, field], X - 1 - l, 1), pltpu.roll(v, X - 1, 1)
        )
        return v + diffusion * (low + high + left + right - 4.0 * v)

    for l in range(L):
        adv_ref[l] = smooth(l, 0, t_ref[l]) + gain_ref[l]
        hum_ref[l] = smooth(l, 1, q_ref[l])
    out_ref[...] = slot_ref[:, 0:CAP, :]


def on_device(t, q, c, sun, lit, owner, table, cond, planck, insol):
    vmem, scratch = pl.BlockSpec(memory_space=pltpu.VMEM), pltpu.VMEM
    field = scratch((L, R, X), f32)
    levels = scratch((L, GP, W2), bf16)
    state = scratch((GP, W2), bf16)
    own = owner[0, :, 0]
    earlier = jnp.arange(R)[None, :] < jnp.arange(R)[:, None]
    rank = jnp.sum(jnp.logical_and(own[:, None] == own[None, :], earlier), axis=1)
    place = (own * 8 + rank).astype(f32)[None]
    gain, halo, slots = pl.pallas_call(
        kernel,
        out_shape=(
            jax.ShapeDtypeStruct((L, R, X), f32),
            jax.ShapeDtypeStruct((4, 2, R, X), f32),
            jax.ShapeDtypeStruct((N_GX, 8, X), f32),
        ),
        in_specs=[vmem] * 4 + [pl.BlockSpec(memory_space=pltpu.SMEM)] + [vmem] * 5,
        out_specs=(vmem,) * 3,
        scratch_shapes=[
            field, field, field, scratch((L + 1, R, X), f32), scratch((L, NT, R, X), f32),
            scratch((L, GP, KW), bf16), scratch((GP, X), bf16), scratch((GP, X), f32),
            levels, levels, scratch((L + 1, GP, W2), bf16), scratch((L + 1, GP, W2), bf16),
            scratch((L, 16, W2), bf16), scratch((L, 16, W2), bf16),
            scratch((32 * R, X), f32), scratch((32, W2), f32), scratch((R, X), f32),
            scratch((R, X), f32), scratch((CH, GP, W2), bf16), state, state, state,
            scratch((16, W2), bf16),
            scratch((2, 2, R, X), f32), scratch((2, 2, R, X), f32),
            scratch((2, 2, R, X), f32), scratch((2, 2, R, X), f32),
            scratch((N_GX, 8, X), f32), scratch((N_GX, 8, X), f32),
            pltpu.SemaphoreType.DMA((4,)), pltpu.SemaphoreType.DMA((4,)),
            pltpu.SemaphoreType.DMA((N_GX,)), pltpu.SemaphoreType.DMA((N_GX,)),
        ],
        compiler_params=pltpu.CompilerParams(
            collective_id=0, has_side_effects=True, vmem_limit_bytes=56 * 2**20
        ),
    )(t, q, c, sun, lit, place, table, cond[None], planck[None], insol[None])
    adv, hum, filled = pl.pallas_call(
        finish,
        out_shape=(
            jax.ShapeDtypeStruct((L, R, X), f32),
            jax.ShapeDtypeStruct((L, R, X), f32),
            jax.ShapeDtypeStruct((N_GX, CAP, X), f32),
        ),
        in_specs=[vmem] * 5,
        out_specs=(vmem,) * 3,
        compiler_params=pltpu.CompilerParams(vmem_limit_bytes=16 * 2**20),
    )(t, q, gain, halo, slots)
    return adv, hum, filled[None, None]


def solution(mesh):
    placed = (
        P(None, "gy", "gx"),
        P(None, "gy", "gx"),
        P(None, "gy", "gx"),
        P("gy", "gx"),
        P("gx", "gy"),
        P("gx", "gy", None),
        P(),
        P(),
        P(),
        P(),
    )
    return jax.shard_map(
        on_device,
        mesh=mesh,
        in_specs=placed,
        out_specs=(P(None, "gy", "gx"), P(None, "gy", "gx"), P("gy", "gx", None, None, None)),
        check_vma=False,
    )
```

```python
import jax
import jax.numpy as jnp
from jax import lax
from jax.experimental import pallas as pl
from jax.experimental.pallas import tpu as pltpu
from jax.sharding import PartitionSpec as P

L, G, GP, NT, NQ, R, X = 30, 140, 144, 16, 8, 32, 128
NC = GP // 16
KW = 144
W2 = 2 * X
PAIRS = R // 2
CAP = 4
N_GX, N_GY = 16, 8
CH = 10
NK = L // CH
diffusion = 0.2
diffusivity = 1.66
SCALE = -diffusivity * 1.4426950408889634
f32, bf16 = jnp.float32, jnp.bfloat16


def kernel(
    t_ref, q_ref, c_ref, sun_ref, lit_ref, own_ref, tab_ref, cond_ref, planck_ref, insol_ref,
    adv_ref, hum_ref, slot_ref,
    hp, cb, ss, ds, th, tabs, pg, qg, tr_a, tr_b, pd_a, pd_b, zacc, bacc, hk, hz, inc, sf,
    xb, Es, Ss, Fs, iv, nsend, nrecv, esend, erecv, ssend, srecv,
    halo_out, halo_in, slot_out, slot_in,
):
    gx, gy = lax.axis_index("gx"), lax.axis_index("gy")
    barrier = pltpu.get_barrier_semaphore()
    mates = [{"gx": lax.rem(gx + d, N_GX), "gy": gy} for d in range(1, N_GX)]
    beside = [{"gx": gx, "gy": lax.rem(gy + d, N_GY)} for d in (1, N_GY - 1)]
    for one_device in mates + beside:
        pl.semaphore_signal(barrier, inc=1, device_id=one_device, device_id_type=pl.DeviceIdType.MESH)

    trs, pds = (tr_a, tr_b), (pd_a, pd_b)

    eye = lax.broadcasted_iota(jnp.int32, (GP, G), 0) == lax.broadcasted_iota(jnp.int32, (GP, G), 1)

    def column(ref):
        return jnp.sum(jnp.where(eye, ref[...], 0.0), axis=1, keepdims=True)

    ccol = column(cond_ref) * SCALE
    psum, qsum = jnp.sum(planck_ref[...]), jnp.sum(insol_ref[...])
    pg[...] = jnp.broadcast_to(column(planck_ref), (GP, X)).astype(bf16)
    qg[...] = jnp.broadcast_to(column(insol_ref), (GP, X))
    lane16 = lax.broadcasted_iota(jnp.int32, (GP, 16), 1)
    chi = ccol.astype(bf16).astype(f32)
    cext = jnp.where(lane16 == 0, chi, jnp.where(lane16 == 1, ccol - chi, 0.0)).astype(bf16)
    lane = lax.broadcasted_iota(jnp.int32, (R, X), 1)
    line = lax.broadcasted_iota(jnp.int32, (R, X), 0)
    nsend[...] = jnp.zeros_like(nsend)
    ds[0] = jnp.zeros((R, X), f32)

    def prepare(l, edges):
        tabs[l, :, 0:NT * NQ] = jnp.concatenate(
            [tab_ref[l].astype(f32) * SCALE, jnp.zeros((GP - G, NT * NQ), f32)], axis=0
        ).astype(bf16)
        tabs[l, :, NT * NQ:KW] = cext
        warm, wet = t_ref[l], q_ref[l]
        t = warm.astype(bf16).astype(f32)
        tp = jnp.clip((t + 3.0) * ((NT - 1.0) / 6.0), 0.0, NT - 1.0)
        for i in range(NT):
            th[l, i] = jnp.maximum(0.0, 1.0 - jnp.abs(tp - float(i)))
        s = 1.0 + 0.25 * t
        ss[l] = s
        ds[l] = edges[4] - s
        hp[l] = jnp.clip(wet.astype(bf16).astype(f32) * (NQ - 1.0), 0.0, NQ - 1.0)
        cb[l] = c_ref[l].astype(bf16).astype(f32)
        here = lane == l
        out = []
        for field, v in enumerate((warm, wet)):
            nsend[0, field, pl.ds(l, 1), :] = v[0:1]
            nsend[1, field, pl.ds(l, 1), :] = v[R - 1:R]
            out.append(jnp.where(here, pltpu.roll(v, l, 1), edges[2 * field]))
            out.append(jnp.where(here, pltpu.roll(v, l + 1, 1), edges[2 * field + 1]))
        return tuple(out) + (s,)

    none = jnp.zeros((R, X), f32)
    edges = lax.fori_loop(0, L, prepare, (none,) * 5)
    ds[L] = none
    for field in range(2):
        for side in range(2):
            esend[side, field] = edges[2 * field + side]

    i8 = lax.broadcasted_iota(jnp.int32, (NQ, W2), 0).astype(f32)
    ex = (lax.broadcasted_iota(jnp.int32, (16, W2), 0) < 2).astype(f32)
    lr = lax.broadcasted_iota(jnp.int32, (32, 16 * L), 0)
    lc = lax.broadcasted_iota(jnp.int32, (32, 16 * L), 1) >> 4
    selz = jnp.where(
        lr == L, (lc == L - 1).astype(f32), (lc == lr - 1).astype(f32) - (lc == lr).astype(f32)
    ).astype(bf16)
    selb = jnp.where(lr < L, (lc == lr + 1).astype(f32) - (lc == lr).astype(f32), 0.0).astype(bf16)

    def tree(v):
        parts = [v[16 * i:16 * i + 16] for i in range(NC)]
        while len(parts) > 1:
            parts = [a + b for a, b in zip(parts[0::2], parts[1::2])] + (
                [parts[-1]] if len(parts) % 2 else []
            )
        return parts[0]

    def row(ref, r0, *at):
        return jnp.concatenate(
            [ref[(*at, pl.ds(r0, 1), slice(None))], ref[(*at, pl.ds(r0 + 1, 1), slice(None))]], axis=1
        )

    def both(v):
        return jnp.concatenate([v, v], axis=1)

    def depth(p, l, j):
        r0 = 2 * p
        hh = jnp.maximum(0.0, 1.0 - jnp.abs(row(hp, r0, l) - i8))
        w = [row(th, r0, l, i) * hh for i in range(NT)]
        w = [jnp.concatenate(w[2 * i:2 * i + 2], axis=0).astype(bf16) for i in range(NT // 2)]
        w.append((ex * row(cb, r0, l)).astype(bf16))
        xb[j] = jnp.dot(
            tabs[l], jnp.concatenate(w, axis=0), preferred_element_type=f32
        ).astype(bf16)

    def start(p):
        r0 = 2 * p
        sun = row(sun_ref, r0)
        lit = jnp.concatenate(
            [jnp.full((1, X), lit_ref[0, r0 + k].astype(f32)) for k in range(2)], axis=1
        )
        iv[...] = jnp.broadcast_to(
            (1.0 / diffusivity) / sun.astype(bf16).astype(f32), (16, W2)
        ).astype(bf16)
        light = (sun * lit).astype(bf16).astype(f32)
        for k in range(2):
            inc[pl.ds(r0 + k, 1), :] = light[:, X * k:X * k + X]
        Es[...] = both(pg[...]) * row(ds, r0, 0).astype(bf16)
        Ss[...] = (both(qg[...]) * light).astype(bf16)

    def down(p, k, par):
        r0 = 2 * p
        E, S = Es[...], Ss[...]
        inv = jnp.concatenate([iv[...]] * NC, axis=0)
        for j in range(CH):
            l = k * CH + j
            x = xb[j]
            trl = jnp.exp2(x)
            trs[par][l] = trl
            down_part = trl * E
            S = S * jnp.exp2(x * inv)
            zacc[l] = tree(down_part + S)
            step = both(pg[...]) * row(ds, r0, l + 1).astype(bf16)
            pds[par][l + 1] = step
            E = down_part + step
        Es[...] = E
        Ss[...] = S

    def up(k, par):
        F = Fs[...]
        for j in range(CH):
            l = L - 1 - (k * CH + j)
            up_part = trs[par][l] * F
            bacc[l] = tree(up_part)
            F = up_part - pds[par][l]
        Fs[...] = F

    def down_sums(p):
        h = jnp.dot(selz, zacc[...].reshape(16 * L, W2), preferred_element_type=f32)
        hz[...] = h
        for k in range(2):
            sf[pl.ds(2 * p + k, 1), :] = h[L:L + 1, X * k:X * k + X]

    def up_sums(p):
        h = hz[...] + jnp.dot(selb, bacc[...].reshape(16 * L, W2), preferred_element_type=f32)
        for k in range(2):
            hk[pl.ds(2 * p + k, 32, stride=32), :] = h[:, X * k:X * k + X]

    def chunks(body):
        def step(k, carry):
            body(k)
            return carry

        lax.fori_loop(0, NK, step, 0)

    def next_and_down(p, k, par):
        n = p * NK + k + 1
        pn, kn = lax.rem(lax.div(n, NK), PAIRS), lax.rem(n, NK)
        down(p, k, par)
        for j in range(CH):
            depth(pn, kn * CH + j, j)

    def whole(p, par):
        start(p)
        Fs[...] = jnp.zeros((GP, W2), bf16)

        def body(k):
            up(k, 1 - par)
            next_and_down(p, k, par)

        chunks(body)
        up_sums(p - 1)
        down_sums(p)

    for ref in pds:
        ref[0] = jnp.zeros((GP, W2), bf16)
    for j in range(CH):
        depth(0, j, j)
    start(0)
    chunks(lambda k: next_and_down(0, k, 0))
    down_sums(0)

    pl.semaphore_wait(barrier, N_GX + 1)
    west, east = {"gx": lax.rem(gx + N_GX - 1, N_GX), "gy": gy}, {"gx": lax.rem(gx + 1, N_GX), "gy": gy}
    south, north = {"gx": gx, "gy": lax.rem(gy + N_GY - 1, N_GY)}, {"gx": gx, "gy": lax.rem(gy + 1, N_GY)}
    halos = []
    for n, (src, dst, target) in enumerate((
        (esend.at[0], erecv.at[1], west), (esend.at[1], erecv.at[0], east),
        (nsend.at[0], nrecv.at[1], south), (nsend.at[1], nrecv.at[0], north),
    )):
        halos.append(pltpu.make_async_remote_copy(
            src_ref=src, dst_ref=dst, send_sem=halo_out.at[n], recv_sem=halo_in.at[n],
            device_id=target, device_id_type=pl.DeviceIdType.MESH,
        ))
        halos[-1].start()

    def two(i, carry):
        whole(2 * i + 1, 1)
        whole(2 * i + 2, 0)
        return carry

    lax.fori_loop(0, (PAIRS - 2) // 2, two, 0)
    whole(PAIRS - 1, 1)

    surface = (sf[...] + psum * ss[L - 1]) * (1.0 / G)
    own_row = own_ref[...].astype(f32)
    er = lax.broadcasted_iota(jnp.int32, (R, R), 0)
    ec = lax.broadcasted_iota(jnp.int32, (R, R), 1)
    own = jnp.sum(jnp.where(er == ec, own_row, 0.0), axis=1, keepdims=True)
    rank = jnp.sum(
        jnp.where(jnp.logical_and(er < ec, own == own_row), 1.0, 0.0), axis=0, keepdims=True
    )
    pick = lax.broadcasted_iota(jnp.int32, (8 * N_GX, R), 0).astype(f32) == own_row * 8.0 + rank
    slots = jnp.dot(
        pick.astype(f32), surface, precision=lax.Precision.HIGHEST, preferred_element_type=f32
    )
    ssend[...] = slots.reshape(N_GX, 8, X)
    sends = []
    for d in range(1, N_GX):
        to = lax.rem(gx + d, N_GX)
        sends.append(pltpu.make_async_remote_copy(
            src_ref=ssend.at[to], dst_ref=srecv.at[gx], send_sem=slot_out.at[d],
            recv_sem=slot_in.at[d], device_id={"gx": to, "gy": gy},
            device_id_type=pl.DeviceIdType.MESH,
        ))
        sends[-1].start()

    Fs[...] = jnp.zeros((GP, W2), bf16)
    chunks(lambda k: up(k, 1))
    up_sums(PAIRS - 1)

    hk[0:R] = hk[0:R] + qsum * inc[...]
    for copy in halos:
        copy.wait()
    inside_w = (gx > 0).astype(f32)
    inside_e = (gx < N_GX - 1).astype(f32)
    inside_s = (gy > 0).astype(f32)
    inside_n = (gy < N_GY - 1).astype(f32)

    def smooth(l, field, v):
        low = jnp.where(line == 0, nrecv[0, field, pl.ds(l, 1), :] * inside_s, pltpu.roll(v, 1, 0))
        high = jnp.where(
            line == R - 1, nrecv[1, field, pl.ds(l, 1), :] * inside_n, pltpu.roll(v, R - 1, 0)
        )
        left = jnp.where(
            lane == 0, pltpu.roll(erecv[0, field], lax.rem(X - l, X), 1) * inside_w, pltpu.roll(v, 1, 1)
        )
        right = jnp.where(
            lane == X - 1, pltpu.roll(erecv[1, field], X - 1 - l, 1) * inside_e,
            pltpu.roll(v, X - 1, 1),
        )
        return v + diffusion * (low + high + left + right - 4.0 * v)

    def last(l, carry):
        gain = hk[pl.ds(pl.multiple_of(R * l, R), R), :] + psum * (ds[l] - ds[l + 1])
        adv_ref[l] = smooth(l, 0, t_ref[l]) + gain * (2.0 / G)
        hum_ref[l] = smooth(l, 1, q_ref[l])
        return carry

    lax.fori_loop(0, L, last, 0)
    for copy in sends:
        copy.wait()
    srecv[gx] = ssend[gx]
    slot_ref[...] = srecv[:, 0:CAP, :]


def on_device(t, q, c, sun, lit, owner, table, cond, planck, insol):
    vmem, scratch = pl.BlockSpec(memory_space=pltpu.VMEM), pltpu.VMEM
    field = scratch((L, R, X), f32)
    levels = scratch((L, GP, W2), bf16)
    state = scratch((GP, W2), bf16)
    out = pl.pallas_call(
        kernel,
        out_shape=(
            jax.ShapeDtypeStruct((L, R, X), f32),
            jax.ShapeDtypeStruct((L, R, X), f32),
            jax.ShapeDtypeStruct((N_GX, CAP, X), f32),
        ),
        in_specs=[vmem] * 4 + [pl.BlockSpec(memory_space=pltpu.SMEM)] + [vmem] * 5,
        out_specs=(vmem,) * 3,
        scratch_shapes=[
            field, field, field, scratch((L + 1, R, X), f32), scratch((L, NT, R, X), f32),
            scratch((L, GP, KW), bf16), scratch((GP, X), bf16), scratch((GP, X), f32),
            levels, levels, scratch((L + 1, GP, W2), bf16), scratch((L + 1, GP, W2), bf16),
            scratch((L, 16, W2), bf16), scratch((L, 16, W2), bf16),
            scratch((32 * R, X), f32), scratch((32, W2), f32), scratch((R, X), f32),
            scratch((R, X), f32), scratch((CH, GP, W2), bf16), state, state, state,
            scratch((16, W2), bf16),
            scratch((2, 2, R, X), f32), scratch((2, 2, R, X), f32),
            scratch((2, 2, R, X), f32), scratch((2, 2, R, X), f32),
            scratch((N_GX, 8, X), f32), scratch((N_GX, 8, X), f32),
            pltpu.SemaphoreType.DMA((4,)), pltpu.SemaphoreType.DMA((4,)),
            pltpu.SemaphoreType.DMA((N_GX,)), pltpu.SemaphoreType.DMA((N_GX,)),
        ],
        compiler_params=pltpu.CompilerParams(
            collective_id=0, has_side_effects=True, vmem_limit_bytes=56 * 2**20
        ),
    )(t, q, c, sun, lit, owner.reshape(1, R), table, cond[None], planck[None], insol[None])
    return out[0], out[1], out[2][None, None]


def solution(mesh):
    placed = (
        P(None, "gy", "gx"),
        P(None, "gy", "gx"),
        P(None, "gy", "gx"),
        P("gy", "gx"),
        P("gx", "gy"),
        P("gx", "gy", None),
        P(),
        P(),
        P(),
        P(),
    )
    return jax.shard_map(
        on_device,
        mesh=mesh,
        in_specs=placed,
        out_specs=(P(None, "gy", "gx"), P(None, "gy", "gx"), P("gy", "gx", None, None, None)),
        check_vma=False,
    )
```

```python
import jax
import jax.numpy as jnp
from jax import lax
from jax.experimental import pallas as pl
from jax.experimental.pallas import tpu as pltpu
from jax.sharding import PartitionSpec as P

L, G, GP, NT, NQ, R, X = 30, 140, 144, 16, 8, 32, 128
NC = GP // 16
KW = 144
W2 = 2 * X
PAIRS = R // 2
CAP = 4
N_GX, N_GY = 16, 8
CH = 10
NK = L // CH
diffusion = 0.2
diffusivity = 1.66
SCALE = -diffusivity * 1.4426950408889634
f32, bf16 = jnp.float32, jnp.bfloat16


def kernel(
    t_ref, q_ref, c_ref, sun_ref, lit_ref, own_ref, tab_ref, cond_ref, planck_ref, insol_ref,
    gain_ref, halo_ref, slot_ref,
    hp, cb, ss, ds, th, tabs, pg, qg, tr_a, tr_b, pd_a, pd_b, zacc, bacc, hk, hz, inc, sf,
    xb, Es, Ss, Fs, iv, nsend, nrecv, esend, erecv, ssend, srecv,
    halo_out, halo_in, slot_out, slot_in,
):
    gx, gy = lax.axis_index("gx"), lax.axis_index("gy")
    barrier = pltpu.get_barrier_semaphore()
    mates = [{"gx": lax.rem(gx + d, N_GX), "gy": gy} for d in range(1, N_GX)]
    beside = [{"gx": gx, "gy": lax.rem(gy + d, N_GY)} for d in (1, N_GY - 1)]
    for one_device in mates + beside:
        pl.semaphore_signal(barrier, inc=1, device_id=one_device, device_id_type=pl.DeviceIdType.MESH)

    trs, pds = (tr_a, tr_b), (pd_a, pd_b)

    eye = lax.broadcasted_iota(jnp.int32, (GP, G), 0) == lax.broadcasted_iota(jnp.int32, (GP, G), 1)

    def column(ref):
        return jnp.sum(jnp.where(eye, ref[...], 0.0), axis=1, keepdims=True)

    ccol = column(cond_ref) * SCALE
    psum, qsum = jnp.sum(planck_ref[...]), jnp.sum(insol_ref[...])
    pg[...] = jnp.broadcast_to(column(planck_ref), (GP, X)).astype(bf16)
    qg[...] = jnp.broadcast_to(column(insol_ref), (GP, X))
    lane16 = lax.broadcasted_iota(jnp.int32, (GP, 16), 1)
    chi = ccol.astype(bf16).astype(f32)
    cext = jnp.where(lane16 == 0, chi, jnp.where(lane16 == 1, ccol - chi, 0.0)).astype(bf16)
    lane = lax.broadcasted_iota(jnp.int32, (R, X), 1)
    nsend[...] = jnp.zeros_like(nsend)
    ds[0] = jnp.zeros((R, X), f32)

    def prepare(l, edges):
        tabs[l, :, 0:NT * NQ] = jnp.concatenate(
            [tab_ref[l].astype(f32) * SCALE, jnp.zeros((GP - G, NT * NQ), f32)], axis=0
        ).astype(bf16)
        tabs[l, :, NT * NQ:KW] = cext
        warm, wet = t_ref[l], q_ref[l]
        t = warm.astype(bf16).astype(f32)
        tp = jnp.clip((t + 3.0) * ((NT - 1.0) / 6.0), 0.0, NT - 1.0)
        for i in range(NT):
            th[l, i] = jnp.maximum(0.0, 1.0 - jnp.abs(tp - float(i)))
        s = 1.0 + 0.25 * t
        ss[l] = s
        ds[l] = edges[4] - s
        hp[l] = jnp.clip(wet.astype(bf16).astype(f32) * (NQ - 1.0), 0.0, NQ - 1.0)
        cb[l] = c_ref[l].astype(bf16).astype(f32)
        here = lane == l
        out = []
        for field, v in enumerate((warm, wet)):
            nsend[0, field, pl.ds(l, 1), :] = v[0:1]
            nsend[1, field, pl.ds(l, 1), :] = v[R - 1:R]
            out.append(jnp.where(here, pltpu.roll(v, l, 1), edges[2 * field]))
            out.append(jnp.where(here, pltpu.roll(v, l + 1, 1), edges[2 * field + 1]))
        return tuple(out) + (s,)

    none = jnp.zeros((R, X), f32)
    edges = lax.fori_loop(0, L, prepare, (none,) * 5)
    ds[L] = none
    for field in range(2):
        for side in range(2):
            esend[side, field] = edges[2 * field + side]

    i8 = lax.broadcasted_iota(jnp.int32, (NQ, W2), 0).astype(f32)
    ex = (lax.broadcasted_iota(jnp.int32, (16, W2), 0) < 2).astype(f32)
    lr = lax.broadcasted_iota(jnp.int32, (32, 16 * L), 0)
    lc = lax.broadcasted_iota(jnp.int32, (32, 16 * L), 1) >> 4
    selz = jnp.where(
        lr == L, (lc == L - 1).astype(f32), (lc == lr - 1).astype(f32) - (lc == lr).astype(f32)
    ).astype(bf16)
    selb = jnp.where(lr < L, (lc == lr + 1).astype(f32) - (lc == lr).astype(f32), 0.0).astype(bf16)

    def tree(v):
        parts = [v[16 * i:16 * i + 16] for i in range(NC)]
        while len(parts) > 1:
            parts = [a + b for a, b in zip(parts[0::2], parts[1::2])] + (
                [parts[-1]] if len(parts) % 2 else []
            )
        return parts[0]

    def row(ref, r0, *at):
        return jnp.concatenate(
            [ref[(*at, pl.ds(r0, 1), slice(None))], ref[(*at, pl.ds(r0 + 1, 1), slice(None))]], axis=1
        )

    def both(v):
        return jnp.concatenate([v, v], axis=1)

    def depth(p, l, j):
        r0 = 2 * p
        hh = jnp.maximum(0.0, 1.0 - jnp.abs(row(hp, r0, l) - i8))
        w = [row(th, r0, l, i) * hh for i in range(NT)]
        w = [jnp.concatenate(w[2 * i:2 * i + 2], axis=0).astype(bf16) for i in range(NT // 2)]
        w.append((ex * row(cb, r0, l)).astype(bf16))
        xb[j] = jnp.dot(
            tabs[l], jnp.concatenate(w, axis=0), preferred_element_type=f32
        ).astype(bf16)

    def start(p):
        r0 = 2 * p
        sun = row(sun_ref, r0)
        lit = jnp.concatenate(
            [jnp.full((1, X), lit_ref[0, r0 + k].astype(f32)) for k in range(2)], axis=1
        )
        iv[...] = jnp.broadcast_to(
            (1.0 / diffusivity) / sun.astype(bf16).astype(f32), (16, W2)
        ).astype(bf16)
        light = (sun * lit).astype(bf16).astype(f32)
        for k in range(2):
            inc[pl.ds(r0 + k, 1), :] = light[:, X * k:X * k + X]
        Es[...] = both(pg[...]) * row(ds, r0, 0).astype(bf16)
        Ss[...] = (both(qg[...]) * light).astype(bf16)

    def down(p, k, par):
        r0 = 2 * p
        E, S = Es[...], Ss[...]
        inv = jnp.concatenate([iv[...]] * NC, axis=0)
        for j in range(CH):
            l = k * CH + j
            x = xb[j]
            trl = jnp.exp2(x)
            trs[par][l] = trl
            down_part = trl * E
            S = S * jnp.exp2(x * inv)
            zacc[l] = tree(down_part + S)
            step = both(pg[...]) * row(ds, r0, l + 1).astype(bf16)
            pds[par][l + 1] = step
            E = down_part + step
        Es[...] = E
        Ss[...] = S

    def up(k, par):
        F = Fs[...]
        for j in range(CH):
            l = L - 1 - (k * CH + j)
            up_part = trs[par][l] * F
            bacc[l] = tree(up_part)
            F = up_part - pds[par][l]
        Fs[...] = F

    def down_sums(p):
        h = jnp.dot(selz, zacc[...].reshape(16 * L, W2), preferred_element_type=f32)
        hz[...] = h
        for k in range(2):
            sf[pl.ds(2 * p + k, 1), :] = h[L:L + 1, X * k:X * k + X]

    def up_sums(p):
        h = hz[...] + jnp.dot(selb, bacc[...].reshape(16 * L, W2), preferred_element_type=f32)
        for k in range(2):
            hk[pl.ds(2 * p + k, 32, stride=32), :] = h[:, X * k:X * k + X]

    def chunks(body):
        def step(k, carry):
            body(k)
            return carry

        lax.fori_loop(0, NK, step, 0)

    def next_and_down(p, k, par):
        n = p * NK + k + 1
        pn, kn = lax.rem(lax.div(n, NK), PAIRS), lax.rem(n, NK)
        down(p, k, par)
        for j in range(CH):
            depth(pn, kn * CH + j, j)

    def whole(p, par):
        start(p)
        Fs[...] = jnp.zeros((GP, W2), bf16)

        def body(k):
            up(k, 1 - par)
            next_and_down(p, k, par)

        chunks(body)
        up_sums(p - 1)
        down_sums(p)

    for ref in pds:
        ref[0] = jnp.zeros((GP, W2), bf16)
    for j in range(CH):
        depth(0, j, j)
    start(0)
    chunks(lambda k: next_and_down(0, k, 0))
    down_sums(0)

    pl.semaphore_wait(barrier, N_GX + 1)
    west, east = {"gx": lax.rem(gx + N_GX - 1, N_GX), "gy": gy}, {"gx": lax.rem(gx + 1, N_GX), "gy": gy}
    south, north = {"gx": gx, "gy": lax.rem(gy + N_GY - 1, N_GY)}, {"gx": gx, "gy": lax.rem(gy + 1, N_GY)}
    halos = []
    for n, (src, dst, target) in enumerate((
        (esend.at[0], erecv.at[1], west), (esend.at[1], erecv.at[0], east),
        (nsend.at[0], nrecv.at[1], south), (nsend.at[1], nrecv.at[0], north),
    )):
        halos.append(pltpu.make_async_remote_copy(
            src_ref=src, dst_ref=dst, send_sem=halo_out.at[n], recv_sem=halo_in.at[n],
            device_id=target, device_id_type=pl.DeviceIdType.MESH,
        ))
        halos[-1].start()

    def two(i, carry):
        whole(2 * i + 1, 1)
        whole(2 * i + 2, 0)
        return carry

    lax.fori_loop(0, (PAIRS - 2) // 2, two, 0)
    whole(PAIRS - 1, 1)

    surface = (sf[...] + psum * ss[L - 1]) * (1.0 / G)
    own_row = own_ref[...].astype(f32)
    er = lax.broadcasted_iota(jnp.int32, (R, R), 0)
    ec = lax.broadcasted_iota(jnp.int32, (R, R), 1)
    own = jnp.sum(jnp.where(er == ec, own_row, 0.0), axis=1, keepdims=True)
    rank = jnp.sum(
        jnp.where(jnp.logical_and(er < ec, own == own_row), 1.0, 0.0), axis=0, keepdims=True
    )
    pick = lax.broadcasted_iota(jnp.int32, (8 * N_GX, R), 0).astype(f32) == own_row * 8.0 + rank
    slots = jnp.dot(
        pick.astype(f32), surface, precision=lax.Precision.HIGHEST, preferred_element_type=f32
    )
    ssend[...] = slots.reshape(N_GX, 8, X)
    sends = []
    for d in range(1, N_GX):
        to = lax.rem(gx + d, N_GX)
        sends.append(pltpu.make_async_remote_copy(
            src_ref=ssend.at[to], dst_ref=srecv.at[gx], send_sem=slot_out.at[d],
            recv_sem=slot_in.at[d], device_id={"gx": to, "gy": gy},
            device_id_type=pl.DeviceIdType.MESH,
        ))
        sends[-1].start()

    Fs[...] = jnp.zeros((GP, W2), bf16)
    chunks(lambda k: up(k, 1))
    up_sums(PAIRS - 1)

    hk[0:R] = hk[0:R] + qsum * inc[...]
    for l in range(L):
        gain_ref[l] = (hk[R * l:R * l + R] + psum * (ds[l] - ds[l + 1])) * (2.0 / G)
    for copy in halos:
        copy.wait()
    halo_ref[0] = erecv[0] * (gx > 0).astype(f32)
    halo_ref[1] = erecv[1] * (gx < N_GX - 1).astype(f32)
    halo_ref[2] = nrecv[0] * (gy > 0).astype(f32)
    halo_ref[3] = nrecv[1] * (gy < N_GY - 1).astype(f32)
    for copy in sends:
        copy.wait()
    srecv[gx] = ssend[gx]
    slot_ref[...] = srecv[...]


LB = 10


def finish(t_ref, q_ref, gain_ref, halo_ref, slot_ref, adv_ref, hum_ref, out_ref):
    lane = lax.broadcasted_iota(jnp.int32, (R, X), 1)
    line = lax.broadcasted_iota(jnp.int32, (R, X), 0)
    first = pl.program_id(0) * LB

    def smooth(l, field, v):
        low = jnp.where(line == 0, halo_ref[2, field, pl.ds(l, 1), :], pltpu.roll(v, 1, 0))
        high = jnp.where(
            line == R - 1, halo_ref[3, field, pl.ds(l, 1), :], pltpu.roll(v, R - 1, 0)
        )
        left = jnp.where(
            lane == 0, pltpu.roll(halo_ref[0, field], lax.rem(X - l, X), 1), pltpu.roll(v, 1, 1)
        )
        right = jnp.where(
            lane == X - 1, pltpu.roll(halo_ref[1, field], X - 1 - l, 1), pltpu.roll(v, X - 1, 1)
        )
        return v + diffusion * (low + high + left + right - 4.0 * v)

    for j in range(LB):
        adv_ref[j] = smooth(first + j, 0, t_ref[j]) + gain_ref[j]
        hum_ref[j] = smooth(first + j, 1, q_ref[j])
    out_ref[...] = slot_ref[:, 0:CAP, :]


def on_device(t, q, c, sun, lit, owner, table, cond, planck, insol):
    vmem, scratch = pl.BlockSpec(memory_space=pltpu.VMEM), pltpu.VMEM
    field = scratch((L, R, X), f32)
    levels = scratch((L, GP, W2), bf16)
    state = scratch((GP, W2), bf16)
    gain, halo, slots = pl.pallas_call(
        kernel,
        out_shape=(
            jax.ShapeDtypeStruct((L, R, X), f32),
            jax.ShapeDtypeStruct((4, 2, R, X), f32),
            jax.ShapeDtypeStruct((N_GX, 8, X), f32),
        ),
        in_specs=[vmem] * 4 + [pl.BlockSpec(memory_space=pltpu.SMEM)] + [vmem] * 5,
        out_specs=(vmem,) * 3,
        scratch_shapes=[
            field, field, field, scratch((L + 1, R, X), f32), scratch((L, NT, R, X), f32),
            scratch((L, GP, KW), bf16), scratch((GP, X), bf16), scratch((GP, X), f32),
            levels, levels, scratch((L + 1, GP, W2), bf16), scratch((L + 1, GP, W2), bf16),
            scratch((L, 16, W2), bf16), scratch((L, 16, W2), bf16),
            scratch((32 * R, X), f32), scratch((32, W2), f32), scratch((R, X), f32),
            scratch((R, X), f32), scratch((CH, GP, W2), bf16), state, state, state,
            scratch((16, W2), bf16),
            scratch((2, 2, R, X), f32), scratch((2, 2, R, X), f32),
            scratch((2, 2, R, X), f32), scratch((2, 2, R, X), f32),
            scratch((N_GX, 8, X), f32), scratch((N_GX, 8, X), f32),
            pltpu.SemaphoreType.DMA((4,)), pltpu.SemaphoreType.DMA((4,)),
            pltpu.SemaphoreType.DMA((N_GX,)), pltpu.SemaphoreType.DMA((N_GX,)),
        ],
        compiler_params=pltpu.CompilerParams(
            collective_id=0, has_side_effects=True, vmem_limit_bytes=56 * 2**20
        ),
    )(t, q, c, sun, lit, owner.reshape(1, R), table, cond[None], planck[None], insol[None])
    some = pl.BlockSpec((LB, R, X), lambda i: (i, 0, 0))
    adv, hum, filled = pl.pallas_call(
        finish,
        grid=(L // LB,),
        out_shape=(
            jax.ShapeDtypeStruct((L, R, X), f32),
            jax.ShapeDtypeStruct((L, R, X), f32),
            jax.ShapeDtypeStruct((N_GX, CAP, X), f32),
        ),
        in_specs=[
            some, some, some,
            pl.BlockSpec((4, 2, R, X), lambda i: (0, 0, 0, 0)),
            pl.BlockSpec((N_GX, 8, X), lambda i: (0, 0, 0)),
        ],
        out_specs=(some, some, pl.BlockSpec((N_GX, CAP, X), lambda i: (0, 0, 0))),
        compiler_params=pltpu.CompilerParams(vmem_limit_bytes=60 * 2**20),
    )(t, q, gain, halo, slots)
    return adv, hum, filled[None, None]


def solution(mesh):
    placed = (
        P(None, "gy", "gx"),
        P(None, "gy", "gx"),
        P(None, "gy", "gx"),
        P("gy", "gx"),
        P("gx", "gy"),
        P("gx", "gy", None),
        P(),
        P(),
        P(),
        P(),
    )
    return jax.shard_map(
        on_device,
        mesh=mesh,
        in_specs=placed,
        out_specs=(P(None, "gy", "gx"), P(None, "gy", "gx"), P("gy", "gx", None, None, None)),
        check_vma=False,
    )
```

```python
import jax
import jax.numpy as jnp
from jax import lax
from jax.experimental import pallas as pl
from jax.experimental.pallas import tpu as pltpu
from jax.sharding import PartitionSpec as P

L, G, GP, NT, NQ, R, X = 30, 140, 144, 16, 8, 32, 128
NC = GP // 16
KW = 144
W2 = 2 * X
PAIRS = R // 2
CAP = 4
N_GX, N_GY = 16, 8
CH = 10
NK = L // CH
diffusion = 0.2
diffusivity = 1.66
SCALE = -diffusivity * 1.4426950408889634
f32, bf16 = jnp.float32, jnp.bfloat16


def kernel(
    t_ref, q_ref, c_ref, sun_ref, lit_ref, own_ref, tab_ref, cond_ref, planck_ref, insol_ref,
    adv_ref, hum_ref, slot_ref,
    hp, cb, ss, ds, th, tabs, pg, qg, tr_a, tr_b, pd_a, pd_b, zacc, bacc, hk, hz, inc, sf,
    xb, Es, Ss, Fs, iv, nsend, nrecv, esend, erecv, ssend, srecv,
    halo_out, halo_in, slot_out, slot_in,
):
    gx, gy = lax.axis_index("gx"), lax.axis_index("gy")
    barrier = pltpu.get_barrier_semaphore()
    mates = [{"gx": lax.rem(gx + d, N_GX), "gy": gy} for d in range(1, N_GX)]
    beside = [{"gx": gx, "gy": lax.rem(gy + d, N_GY)} for d in (1, N_GY - 1)]
    for one_device in mates + beside:
        pl.semaphore_signal(barrier, inc=1, device_id=one_device, device_id_type=pl.DeviceIdType.MESH)

    trs, pds = (tr_a, tr_b), (pd_a, pd_b)

    eye = lax.broadcasted_iota(jnp.int32, (GP, G), 0) == lax.broadcasted_iota(jnp.int32, (GP, G), 1)

    def column(ref):
        return jnp.sum(jnp.where(eye, ref[...], 0.0), axis=1, keepdims=True)

    ccol = column(cond_ref) * SCALE
    psum, qsum = jnp.sum(planck_ref[...]), jnp.sum(insol_ref[...])
    pg[...] = jnp.broadcast_to(column(planck_ref), (GP, X)).astype(bf16)
    qg[...] = jnp.broadcast_to(column(insol_ref), (GP, X))
    lane16 = lax.broadcasted_iota(jnp.int32, (GP, 16), 1)
    chi = ccol.astype(bf16).astype(f32)
    cext = jnp.where(lane16 == 0, chi, jnp.where(lane16 == 1, ccol - chi, 0.0)).astype(bf16)
    lane = lax.broadcasted_iota(jnp.int32, (R, X), 1)
    line = lax.broadcasted_iota(jnp.int32, (R, X), 0)
    nsend[...] = jnp.zeros_like(nsend)
    ds[0] = jnp.zeros((R, X), f32)

    none = jnp.zeros((R, X), f32)

    def prepare(l, edges):
        tabs[l, :, 0:NT * NQ] = jnp.concatenate(
            [tab_ref[l].astype(f32) * SCALE, jnp.zeros((GP - G, NT * NQ), f32)], axis=0
        ).astype(bf16)
        tabs[l, :, NT * NQ:KW] = cext
        warm, wet = t_ref[l], q_ref[l]
        t = warm.astype(bf16).astype(f32)
        tp = jnp.clip((t + 3.0) * ((NT - 1.0) / 6.0), 0.0, NT - 1.0)
        node = jnp.floor(tp)
        f = tp - node
        below, above = 1.0 - f, none
        for i in range(NT):
            at = node == float(i)
            th[l, i] = jnp.where(at, below, above)
            above = jnp.where(at, f, none)
        s = 1.0 + 0.25 * t
        ss[l] = s
        ds[l] = edges[4] - s
        hp[l] = jnp.clip(wet.astype(bf16).astype(f32) * (NQ - 1.0), 0.0, NQ - 1.0)
        cb[l] = c_ref[l].astype(bf16).astype(f32)
        here = lane == l
        out = []
        for field, v in enumerate((warm, wet)):
            nsend[0, field, pl.ds(l, 1), :] = v[0:1]
            nsend[1, field, pl.ds(l, 1), :] = v[R - 1:R]
            out.append(jnp.where(here, pltpu.roll(v, l, 1), edges[2 * field]))
            out.append(jnp.where(here, pltpu.roll(v, l + 1, 1), edges[2 * field + 1]))
        return tuple(out) + (s,)

    edges = lax.fori_loop(0, L, prepare, (none,) * 5)
    ds[L] = none
    for field in range(2):
        for side in range(2):
            esend[side, field] = edges[2 * field + side]

    i8 = lax.broadcasted_iota(jnp.int32, (NQ, W2), 0).astype(f32)
    ex = (lax.broadcasted_iota(jnp.int32, (16, W2), 0) < 2).astype(f32)
    lr = lax.broadcasted_iota(jnp.int32, (32, 16 * L), 0)
    lc = lax.broadcasted_iota(jnp.int32, (32, 16 * L), 1) >> 4
    selz = jnp.where(
        lr == L, (lc == L - 1).astype(f32), (lc == lr - 1).astype(f32) - (lc == lr).astype(f32)
    ).astype(bf16)
    selb = jnp.where(lr < L, (lc == lr + 1).astype(f32) - (lc == lr).astype(f32), 0.0).astype(bf16)

    def tree(v):
        parts = [v[16 * i:16 * i + 16] for i in range(NC)]
        while len(parts) > 1:
            parts = [a + b for a, b in zip(parts[0::2], parts[1::2])] + (
                [parts[-1]] if len(parts) % 2 else []
            )
        return parts[0]

    def row(ref, r0, *at):
        return jnp.concatenate(
            [ref[(*at, pl.ds(r0, 1), slice(None))], ref[(*at, pl.ds(r0 + 1, 1), slice(None))]], axis=1
        )

    def both(v):
        return jnp.concatenate([v, v], axis=1)

    def depth(p, l, j):
        r0 = 2 * p
        hh = jnp.maximum(0.0, 1.0 - jnp.abs(row(hp, r0, l) - i8))
        w = [row(th, r0, l, i) * hh for i in range(NT)]
        w = [jnp.concatenate(w[2 * i:2 * i + 2], axis=0).astype(bf16) for i in range(NT // 2)]
        w.append((ex * row(cb, r0, l)).astype(bf16))
        xb[j] = jnp.dot(
            tabs[l], jnp.concatenate(w, axis=0), preferred_element_type=f32
        ).astype(bf16)

    def start(p):
        r0 = 2 * p
        sun = row(sun_ref, r0)
        lit = jnp.concatenate(
            [jnp.full((1, X), lit_ref[0, r0 + k].astype(f32)) for k in range(2)], axis=1
        )
        iv[...] = jnp.broadcast_to(
            (1.0 / diffusivity) / sun.astype(bf16).astype(f32), (16, W2)
        ).astype(bf16)
        light = (sun * lit).astype(bf16).astype(f32)
        for k in range(2):
            inc[pl.ds(r0 + k, 1), :] = light[:, X * k:X * k + X]
        Es[...] = both(pg[...]) * row(ds, r0, 0).astype(bf16)
        Ss[...] = (both(qg[...]) * light).astype(bf16)

    def down(p, k, par):
        r0 = 2 * p
        E, S = Es[...], Ss[...]
        inv = jnp.concatenate([iv[...]] * NC, axis=0)
        for j in range(CH):
            l = k * CH + j
            x = xb[j]
            trl = jnp.exp2(x)
            trs[par][l] = trl
            down_part = trl * E
            S = S * jnp.exp2(x * inv)
            zacc[l] = tree(down_part + S)
            step = both(pg[...]) * row(ds, r0, l + 1).astype(bf16)
            pds[par][l + 1] = step
            E = down_part + step
        Es[...] = E
        Ss[...] = S

    def up(k, par):
        F = Fs[...]
        for j in range(CH):
            l = L - 1 - (k * CH + j)
            up_part = trs[par][l] * F
            bacc[l] = tree(up_part)
            F = up_part - pds[par][l]
        Fs[...] = F

    def down_sums(p):
        h = jnp.dot(selz, zacc[...].reshape(16 * L, W2), preferred_element_type=f32)
        hz[...] = h
        for k in range(2):
            sf[pl.ds(2 * p + k, 1), :] = h[L:L + 1, X * k:X * k + X]

    def up_sums(p):
        h = hz[...] + jnp.dot(selb, bacc[...].reshape(16 * L, W2), preferred_element_type=f32)
        for k in range(2):
            hk[pl.ds(2 * p + k, 32, stride=32), :] = h[:, X * k:X * k + X]

    def chunks(body):
        def step(k, carry):
            body(k)
            return carry

        lax.fori_loop(0, NK, step, 0)

    def next_and_down(p, k, par):
        n = p * NK + k + 1
        pn, kn = lax.rem(lax.div(n, NK), PAIRS), lax.rem(n, NK)
        down(p, k, par)
        for j in range(CH):
            depth(pn, kn * CH + j, j)

    def whole(p, par):
        start(p)
        Fs[...] = jnp.zeros((GP, W2), bf16)

        def body(k):
            up(k, 1 - par)
            next_and_down(p, k, par)

        chunks(body)
        up_sums(p - 1)
        down_sums(p)

    for ref in pds:
        ref[0] = jnp.zeros((GP, W2), bf16)
    for j in range(CH):
        depth(0, j, j)
    start(0)
    chunks(lambda k: next_and_down(0, k, 0))
    down_sums(0)

    pl.semaphore_wait(barrier, N_GX + 1)
    west, east = {"gx": lax.rem(gx + N_GX - 1, N_GX), "gy": gy}, {"gx": lax.rem(gx + 1, N_GX), "gy": gy}
    south, north = {"gx": gx, "gy": lax.rem(gy + N_GY - 1, N_GY)}, {"gx": gx, "gy": lax.rem(gy + 1, N_GY)}
    halos = []
    for n, (src, dst, target) in enumerate((
        (esend.at[0], erecv.at[1], west), (esend.at[1], erecv.at[0], east),
        (nsend.at[0], nrecv.at[1], south), (nsend.at[1], nrecv.at[0], north),
    )):
        halos.append(pltpu.make_async_remote_copy(
            src_ref=src, dst_ref=dst, send_sem=halo_out.at[n], recv_sem=halo_in.at[n],
            device_id=target, device_id_type=pl.DeviceIdType.MESH,
        ))
        halos[-1].start()

    def two(i, carry):
        whole(2 * i + 1, 1)
        whole(2 * i + 2, 0)
        return carry

    lax.fori_loop(0, (PAIRS - 2) // 2, two, 0)
    whole(PAIRS - 1, 1)

    surface = (sf[...] + psum * ss[L - 1]) * (1.0 / G)
    own_row = own_ref[...].astype(f32)
    er = lax.broadcasted_iota(jnp.int32, (R, R), 0)
    ec = lax.broadcasted_iota(jnp.int32, (R, R), 1)
    own = jnp.sum(jnp.where(er == ec, own_row, 0.0), axis=1, keepdims=True)
    rank = jnp.sum(
        jnp.where(jnp.logical_and(er < ec, own == own_row), 1.0, 0.0), axis=0, keepdims=True
    )
    pick = lax.broadcasted_iota(jnp.int32, (8 * N_GX, R), 0).astype(f32) == own_row * 8.0 + rank
    slots = jnp.dot(
        pick.astype(f32), surface, precision=lax.Precision.HIGHEST, preferred_element_type=f32
    )
    ssend[...] = slots.reshape(N_GX, 8, X)
    sends = []
    for d in range(1, N_GX):
        to = lax.rem(gx + d, N_GX)
        sends.append(pltpu.make_async_remote_copy(
            src_ref=ssend.at[to], dst_ref=srecv.at[gx], send_sem=slot_out.at[d],
            recv_sem=slot_in.at[d], device_id={"gx": to, "gy": gy},
            device_id_type=pl.DeviceIdType.MESH,
        ))
        sends[-1].start()

    Fs[...] = jnp.zeros((GP, W2), bf16)
    chunks(lambda k: up(k, 1))
    up_sums(PAIRS - 1)

    hk[0:R] = hk[0:R] + qsum * inc[...]
    for copy in halos:
        copy.wait()
    inside_w = (gx > 0).astype(f32)
    inside_e = (gx < N_GX - 1).astype(f32)
    inside_s = (gy > 0).astype(f32)
    inside_n = (gy < N_GY - 1).astype(f32)

    def smooth(l, field, v):
        low = jnp.where(line == 0, nrecv[0, field, pl.ds(l, 1), :] * inside_s, pltpu.roll(v, 1, 0))
        high = jnp.where(
            line == R - 1, nrecv[1, field, pl.ds(l, 1), :] * inside_n, pltpu.roll(v, R - 1, 0)
        )
        left = jnp.where(
            lane == 0, pltpu.roll(erecv[0, field], lax.rem(X - l, X), 1) * inside_w, pltpu.roll(v, 1, 1)
        )
        right = jnp.where(
            lane == X - 1, pltpu.roll(erecv[1, field], X - 1 - l, 1) * inside_e,
            pltpu.roll(v, X - 1, 1),
        )
        return v + diffusion * (low + high + left + right - 4.0 * v)

    def last(i, carry):
        for j in range(5):
            l = 5 * i + j
            gain = hk[pl.ds(pl.multiple_of(R * l, R), R), :] + psum * (ds[l] - ds[l + 1])
            adv_ref[l] = smooth(l, 0, t_ref[l]) + gain * (2.0 / G)
            hum_ref[l] = smooth(l, 1, q_ref[l])
        return carry

    lax.fori_loop(0, L // 5, last, 0)
    for copy in sends:
        copy.wait()
    srecv[gx] = ssend[gx]
    slot_ref[...] = srecv[:, 0:CAP, :]


def on_device(t, q, c, sun, lit, owner, table, cond, planck, insol):
    vmem, scratch = pl.BlockSpec(memory_space=pltpu.VMEM), pltpu.VMEM
    field = scratch((L, R, X), f32)
    levels = scratch((L, GP, W2), bf16)
    state = scratch((GP, W2), bf16)
    out = pl.pallas_call(
        kernel,
        out_shape=(
            jax.ShapeDtypeStruct((L, R, X), f32),
            jax.ShapeDtypeStruct((L, R, X), f32),
            jax.ShapeDtypeStruct((N_GX, CAP, X), f32),
        ),
        in_specs=[vmem] * 4 + [pl.BlockSpec(memory_space=pltpu.SMEM)] + [vmem] * 5,
        out_specs=(vmem,) * 3,
        scratch_shapes=[
            field, field, field, scratch((L + 1, R, X), f32), scratch((L, NT, R, X), f32),
            scratch((L, GP, KW), bf16), scratch((GP, X), bf16), scratch((GP, X), f32),
            levels, levels, scratch((L + 1, GP, W2), bf16), scratch((L + 1, GP, W2), bf16),
            scratch((L, 16, W2), bf16), scratch((L, 16, W2), bf16),
            scratch((32 * R, X), f32), scratch((32, W2), f32), scratch((R, X), f32),
            scratch((R, X), f32), scratch((CH, GP, W2), bf16), state, state, state,
            scratch((16, W2), bf16),
            scratch((2, 2, R, X), f32), scratch((2, 2, R, X), f32),
            scratch((2, 2, R, X), f32), scratch((2, 2, R, X), f32),
            scratch((N_GX, 8, X), f32), scratch((N_GX, 8, X), f32),
            pltpu.SemaphoreType.DMA((4,)), pltpu.SemaphoreType.DMA((4,)),
            pltpu.SemaphoreType.DMA((N_GX,)), pltpu.SemaphoreType.DMA((N_GX,)),
        ],
        compiler_params=pltpu.CompilerParams(
            collective_id=0, has_side_effects=True, vmem_limit_bytes=56 * 2**20
        ),
    )(t, q, c, sun, lit, owner.reshape(1, R), table, cond[None], planck[None], insol[None])
    return out[0], out[1], out[2][None, None]


def solution(mesh):
    placed = (
        P(None, "gy", "gx"),
        P(None, "gy", "gx"),
        P(None, "gy", "gx"),
        P("gy", "gx"),
        P("gx", "gy"),
        P("gx", "gy", None),
        P(),
        P(),
        P(),
        P(),
    )
    return jax.shard_map(
        on_device,
        mesh=mesh,
        in_specs=placed,
        out_specs=(P(None, "gy", "gx"), P(None, "gy", "gx"), P("gy", "gx", None, None, None)),
        check_vma=False,
    )
```

```python
import jax
import jax.numpy as jnp
from jax import lax
from jax.experimental import pallas as pl
from jax.experimental.pallas import tpu as pltpu
from jax.sharding import PartitionSpec as P

L, G, GP, NT, NQ, R, X = 30, 140, 144, 16, 8, 32, 128
NC = GP // 16
KW = 144
W2 = 2 * X
PAIRS = R // 2
CAP = 4
N_GX, N_GY = 16, 8
CH = 10
NK = L // CH
diffusion = 0.2
diffusivity = 1.66
SCALE = -diffusivity * 1.4426950408889634
f32, bf16 = jnp.float32, jnp.bfloat16


def kernel(
    t_ref, q_ref, c_ref, sun_ref, lit_ref, own_ref, tab_ref, cond_ref, planck_ref, insol_ref,
    adv_ref, hum_ref, slot_ref,
    hp, cb, ss, ds, th, tabs, pg, qg, tr_a, tr_b, pd_a, pd_b, zacc, bacc, hk, hz, inc, sf,
    xb, Es, Ss, Fs, iv, nsend, nrecv, esend, erecv, ssend, srecv,
    halo_out, halo_in, slot_out, slot_in,
):
    gx, gy = lax.axis_index("gx"), lax.axis_index("gy")
    barrier = pltpu.get_barrier_semaphore()
    mates = [{"gx": lax.rem(gx + d, N_GX), "gy": gy} for d in range(1, N_GX)]
    beside = [{"gx": gx, "gy": lax.rem(gy + d, N_GY)} for d in (1, N_GY - 1)]
    for one_device in mates + beside:
        pl.semaphore_signal(barrier, inc=1, device_id=one_device, device_id_type=pl.DeviceIdType.MESH)

    trs, pds = (tr_a, tr_b), (pd_a, pd_b)

    eye = lax.broadcasted_iota(jnp.int32, (GP, G), 0) == lax.broadcasted_iota(jnp.int32, (GP, G), 1)

    def column(ref):
        return jnp.sum(jnp.where(eye, ref[...], 0.0), axis=1, keepdims=True)

    ccol = column(cond_ref) * SCALE
    psum, qsum = jnp.sum(planck_ref[...]), jnp.sum(insol_ref[...])
    pg[...] = jnp.broadcast_to(column(planck_ref), (GP, X)).astype(bf16)
    qg[...] = jnp.broadcast_to(column(insol_ref), (GP, X))
    lane16 = lax.broadcasted_iota(jnp.int32, (GP, 16), 1)
    chi = ccol.astype(bf16).astype(f32)
    cext = jnp.where(lane16 == 0, chi, jnp.where(lane16 == 1, ccol - chi, 0.0)).astype(bf16)
    lane = lax.broadcasted_iota(jnp.int32, (R, X), 1)
    line = lax.broadcasted_iota(jnp.int32, (R, X), 0)
    nsend[...] = jnp.zeros_like(nsend)
    ds[0] = jnp.zeros((R, X), f32)

    none = jnp.zeros((R, X), f32)

    def prepare(l, edges):
        tabs[l, :, 0:NT * NQ] = jnp.concatenate(
            [tab_ref[l].astype(f32) * SCALE, jnp.zeros((GP - G, NT * NQ), f32)], axis=0
        ).astype(bf16)
        tabs[l, :, NT * NQ:KW] = cext
        warm, wet = t_ref[l], q_ref[l]
        t = warm.astype(bf16).astype(f32)
        tp = jnp.clip((t + 3.0) * ((NT - 1.0) / 6.0), 0.0, NT - 1.0)
        node = jnp.floor(tp)
        f = tp - node
        below, above = 1.0 - f, none
        for i in range(NT):
            at = node == float(i)
            th[l, i] = jnp.where(at, below, above)
            above = jnp.where(at, f, none)
        s = 1.0 + 0.25 * t
        ss[l] = s
        ds[l] = edges[4] - s
        hp[l] = jnp.clip(wet.astype(bf16).astype(f32) * (NQ - 1.0), 0.0, NQ - 1.0)
        cb[l] = c_ref[l].astype(bf16).astype(f32)
        here = lane == l
        out = []
        for field, v in enumerate((warm, wet)):
            nsend[0, field, pl.ds(l, 1), :] = v[0:1]
            nsend[1, field, pl.ds(l, 1), :] = v[R - 1:R]
            out.append(jnp.where(here, pltpu.roll(v, l, 1), edges[2 * field]))
            out.append(jnp.where(here, pltpu.roll(v, l + 1, 1), edges[2 * field + 1]))
        return tuple(out) + (s,)

    edges = lax.fori_loop(0, L, prepare, (none,) * 5)
    ds[L] = none
    for field in range(2):
        for side in range(2):
            esend[side, field] = edges[2 * field + side]

    i8 = lax.broadcasted_iota(jnp.int32, (NQ, W2), 0).astype(f32)
    ex = (lax.broadcasted_iota(jnp.int32, (16, W2), 0) < 2).astype(f32)
    lr = lax.broadcasted_iota(jnp.int32, (32, 16 * L), 0)
    lc = lax.broadcasted_iota(jnp.int32, (32, 16 * L), 1) >> 4
    selz = jnp.where(
        lr == L, (lc == L - 1).astype(f32), (lc == lr - 1).astype(f32) - (lc == lr).astype(f32)
    ).astype(bf16)
    selb = jnp.where(lr < L, (lc == lr + 1).astype(f32) - (lc == lr).astype(f32), 0.0).astype(bf16)

    def tree(v):
        parts = [v[16 * i:16 * i + 16] for i in range(NC)]
        while len(parts) > 1:
            parts = [a + b for a, b in zip(parts[0::2], parts[1::2])] + (
                [parts[-1]] if len(parts) % 2 else []
            )
        return parts[0]

    def row(ref, r0, *at):
        return jnp.concatenate(
            [ref[(*at, pl.ds(r0, 1), slice(None))], ref[(*at, pl.ds(r0 + 1, 1), slice(None))]], axis=1
        )

    def both(v):
        return jnp.concatenate([v, v], axis=1)

    def depth(p, l, j):
        r0 = 2 * p
        hh = jnp.maximum(0.0, 1.0 - jnp.abs(row(hp, r0, l) - i8))
        w = [row(th, r0, l, i) * hh for i in range(NT)]
        w = [jnp.concatenate(w[2 * i:2 * i + 2], axis=0).astype(bf16) for i in range(NT // 2)]
        w.append((ex * row(cb, r0, l)).astype(bf16))
        xb[j] = jnp.dot(
            tabs[l], jnp.concatenate(w, axis=0), preferred_element_type=f32
        ).astype(bf16)

    def start(p):
        r0 = 2 * p
        sun = row(sun_ref, r0)
        lit = jnp.concatenate(
            [jnp.full((1, X), lit_ref[0, r0 + k].astype(f32)) for k in range(2)], axis=1
        )
        iv[...] = jnp.broadcast_to(
            (1.0 / diffusivity) / sun.astype(bf16).astype(f32), (16, W2)
        ).astype(bf16)
        light = (sun * lit).astype(bf16).astype(f32)
        for k in range(2):
            inc[pl.ds(r0 + k, 1), :] = light[:, X * k:X * k + X]
        Es[...] = both(pg[...]) * row(ds, r0, 0).astype(bf16)
        Ss[...] = (both(qg[...]) * light).astype(bf16)

    def down(p, k, par):
        r0 = 2 * p
        E, S = Es[...], Ss[...]
        inv = jnp.concatenate([iv[...]] * NC, axis=0)
        for j in range(CH):
            l = k * CH + j
            x = xb[j]
            trl = jnp.exp2(x)
            trs[par][l] = trl
            down_part = trl * E
            S = S * jnp.exp2(x * inv)
            zacc[l] = tree(down_part + S)
            step = both(pg[...]) * row(ds, r0, l + 1).astype(bf16)
            pds[par][l + 1] = step
            E = down_part + step
        Es[...] = E
        Ss[...] = S

    def up(k, par):
        F = Fs[...]
        for j in range(CH):
            l = L - 1 - (k * CH + j)
            up_part = trs[par][l] * F
            bacc[l] = tree(up_part)
            F = up_part - pds[par][l]
        Fs[...] = F

    def down_sums(p):
        h = jnp.dot(selz, zacc[...].reshape(16 * L, W2), preferred_element_type=f32)
        hz[...] = h
        for k in range(2):
            sf[pl.ds(2 * p + k, 1), :] = h[L:L + 1, X * k:X * k + X]

    def up_sums(p):
        h = hz[...] + jnp.dot(selb, bacc[...].reshape(16 * L, W2), preferred_element_type=f32)
        for k in range(2):
            hk[pl.ds(2 * p + k, 32, stride=32), :] = h[:, X * k:X * k + X]

    def chunks(body):
        def step(k, carry):
            body(k)
            return carry

        lax.fori_loop(0, NK, step, 0)

    def next_and_down(p, k, par):
        n = p * NK + k + 1
        pn, kn = lax.rem(lax.div(n, NK), PAIRS), lax.rem(n, NK)
        down(p, k, par)
        for j in range(CH):
            depth(pn, kn * CH + j, j)

    def whole(p, par):
        start(p)
        Fs[...] = jnp.zeros((GP, W2), bf16)

        def body(k):
            up(k, 1 - par)
            next_and_down(p, k, par)

        chunks(body)
        up_sums(p - 1)
        down_sums(p)

    for ref in pds:
        ref[0] = jnp.zeros((GP, W2), bf16)
    for j in range(CH):
        depth(0, j, j)
    start(0)
    chunks(lambda k: next_and_down(0, k, 0))
    down_sums(0)

    pl.semaphore_wait(barrier, N_GX + 1)
    west, east = {"gx": lax.rem(gx + N_GX - 1, N_GX), "gy": gy}, {"gx": lax.rem(gx + 1, N_GX), "gy": gy}
    south, north = {"gx": gx, "gy": lax.rem(gy + N_GY - 1, N_GY)}, {"gx": gx, "gy": lax.rem(gy + 1, N_GY)}
    halos = []
    for n, (src, dst, target) in enumerate((
        (esend.at[0], erecv.at[1], west), (esend.at[1], erecv.at[0], east),
        (nsend.at[0], nrecv.at[1], south), (nsend.at[1], nrecv.at[0], north),
    )):
        halos.append(pltpu.make_async_remote_copy(
            src_ref=src, dst_ref=dst, send_sem=halo_out.at[n], recv_sem=halo_in.at[n],
            device_id=target, device_id_type=pl.DeviceIdType.MESH,
        ))
        halos[-1].start()

    def two(i, carry):
        whole(2 * i + 1, 1)
        whole(2 * i + 2, 0)
        return carry

    lax.fori_loop(0, (PAIRS - 2) // 2, two, 0)
    whole(PAIRS - 1, 1)

    surface = (sf[...] + psum * ss[L - 1]) * (1.0 / G)
    own_row = own_ref[...].astype(f32)
    er = lax.broadcasted_iota(jnp.int32, (R, R), 0)
    ec = lax.broadcasted_iota(jnp.int32, (R, R), 1)
    own = jnp.sum(jnp.where(er == ec, own_row, 0.0), axis=1, keepdims=True)
    rank = jnp.sum(
        jnp.where(jnp.logical_and(er < ec, own == own_row), 1.0, 0.0), axis=0, keepdims=True
    )
    pick = lax.broadcasted_iota(jnp.int32, (8 * N_GX, R), 0).astype(f32) == own_row * 8.0 + rank
    slots = jnp.dot(
        pick.astype(f32), surface, precision=lax.Precision.HIGHEST, preferred_element_type=f32
    )
    ssend[...] = slots.reshape(N_GX, 8, X)
    sends = []
    for d in range(1, N_GX):
        to = lax.rem(gx + d, N_GX)
        sends.append(pltpu.make_async_remote_copy(
            src_ref=ssend.at[to], dst_ref=srecv.at[gx], send_sem=slot_out.at[d],
            recv_sem=slot_in.at[d], device_id={"gx": to, "gy": gy},
            device_id_type=pl.DeviceIdType.MESH,
        ))
        sends[-1].start()

    Fs[...] = jnp.zeros((GP, W2), bf16)
    chunks(lambda k: up(k, 1))
    up_sums(PAIRS - 1)

    hk[0:R] = hk[0:R] + qsum * inc[...]
    for copy in halos:
        copy.wait()
    inside_w = (gx > 0).astype(f32)
    inside_e = (gx < N_GX - 1).astype(f32)
    inside_s = (gy > 0).astype(f32)
    inside_n = (gy < N_GY - 1).astype(f32)

    def smooth(l, field, v):
        low = jnp.where(line == 0, nrecv[0, field, pl.ds(l, 1), :] * inside_s, pltpu.roll(v, 1, 0))
        high = jnp.where(
            line == R - 1, nrecv[1, field, pl.ds(l, 1), :] * inside_n, pltpu.roll(v, R - 1, 0)
        )
        left = jnp.where(
            lane == 0, pltpu.roll(erecv[0, field], lax.rem(X - l, X), 1) * inside_w, pltpu.roll(v, 1, 1)
        )
        right = jnp.where(
            lane == X - 1, pltpu.roll(erecv[1, field], X - 1 - l, 1) * inside_e,
            pltpu.roll(v, X - 1, 1),
        )
        return v + diffusion * (low + high + left + right - 4.0 * v)

    def last(i, carry):
        for j in range(5):
            l = 5 * i + j
            gain = hk[pl.ds(pl.multiple_of(R * l, R), R), :] + psum * (ds[l] - ds[l + 1])
            adv_ref[l] = smooth(l, 0, t_ref[l]) + gain * (2.0 / G)
            hum_ref[l] = smooth(l, 1, q_ref[l])
        return carry

    lax.fori_loop(0, L // 5, last, 0)
    for copy in sends:
        copy.wait()
    srecv[gx] = ssend[gx]
    slot_ref[...] = srecv[:, 0:CAP, :]


def hand_over(adv_in, hum_in, slot_in, adv_ref, hum_ref, slot_ref, sems):
    step = L // 3
    copies = [pltpu.make_async_copy(slot_in, slot_ref, sems.at[6])]
    for n in range(3):
        at = pl.ds(n * step, step)
        copies.append(pltpu.make_async_copy(adv_in.at[at], adv_ref.at[at], sems.at[2 * n]))
        copies.append(pltpu.make_async_copy(hum_in.at[at], hum_ref.at[at], sems.at[2 * n + 1]))
    for copy in copies:
        copy.start()
    for copy in copies:
        copy.wait()


def on_device(t, q, c, sun, lit, owner, table, cond, planck, insol):
    vmem, scratch = pl.BlockSpec(memory_space=pltpu.VMEM), pltpu.VMEM
    field = scratch((L, R, X), f32)
    levels = scratch((L, GP, W2), bf16)
    state = scratch((GP, W2), bf16)
    out = pl.pallas_call(
        kernel,
        out_shape=(
            jax.ShapeDtypeStruct((L, R, X), f32),
            jax.ShapeDtypeStruct((L, R, X), f32),
            jax.ShapeDtypeStruct((N_GX, CAP, X), f32),
        ),
        in_specs=[vmem] * 4 + [pl.BlockSpec(memory_space=pltpu.SMEM)] + [vmem] * 5,
        out_specs=(vmem,) * 3,
        scratch_shapes=[
            field, field, field, scratch((L + 1, R, X), f32), scratch((L, NT, R, X), f32),
            scratch((L, GP, KW), bf16), scratch((GP, X), bf16), scratch((GP, X), f32),
            levels, levels, scratch((L + 1, GP, W2), bf16), scratch((L + 1, GP, W2), bf16),
            scratch((L, 16, W2), bf16), scratch((L, 16, W2), bf16),
            scratch((32 * R, X), f32), scratch((32, W2), f32), scratch((R, X), f32),
            scratch((R, X), f32), scratch((CH, GP, W2), bf16), state, state, state,
            scratch((16, W2), bf16),
            scratch((2, 2, R, X), f32), scratch((2, 2, R, X), f32),
            scratch((2, 2, R, X), f32), scratch((2, 2, R, X), f32),
            scratch((N_GX, 8, X), f32), scratch((N_GX, 8, X), f32),
            pltpu.SemaphoreType.DMA((4,)), pltpu.SemaphoreType.DMA((4,)),
            pltpu.SemaphoreType.DMA((N_GX,)), pltpu.SemaphoreType.DMA((N_GX,)),
        ],
        compiler_params=pltpu.CompilerParams(
            collective_id=0, has_side_effects=True, vmem_limit_bytes=56 * 2**20
        ),
    )(t, q, c, sun, lit, owner.reshape(1, R), table, cond[None], planck[None], insol[None])
    anywhere = pl.BlockSpec(memory_space=pl.ANY)
    out = pl.pallas_call(
        hand_over,
        out_shape=tuple(jax.ShapeDtypeStruct(v.shape, f32) for v in out),
        in_specs=[anywhere] * 3,
        out_specs=(anywhere,) * 3,
        scratch_shapes=[pltpu.SemaphoreType.DMA((7,))],
        compiler_params=pltpu.CompilerParams(vmem_limit_bytes=60 * 2**20),
    )(*out)
    return out[0], out[1], out[2][None, None]


def solution(mesh):
    placed = (
        P(None, "gy", "gx"),
        P(None, "gy", "gx"),
        P(None, "gy", "gx"),
        P("gy", "gx"),
        P("gx", "gy"),
        P("gx", "gy", None),
        P(),
        P(),
        P(),
        P(),
    )
    return jax.shard_map(
        on_device,
        mesh=mesh,
        in_specs=placed,
        out_specs=(P(None, "gy", "gx"), P(None, "gy", "gx"), P("gy", "gx", None, None, None)),
        check_vma=False,
    )
```

```python
import jax
import jax.numpy as jnp
from jax import lax
from jax.experimental import pallas as pl
from jax.experimental.pallas import tpu as pltpu
from jax.sharding import PartitionSpec as P

L, G, GP, NT, NQ, R, X = 30, 140, 144, 16, 8, 32, 128
NC = GP // 16
KW = 144
W2 = 2 * X
PAIRS = R // 2
CAP = 4
N_GX, N_GY = 16, 8
CH = 10
NK = L // CH
diffusion = 0.2
diffusivity = 1.66
SCALE = -diffusivity * 1.4426950408889634
f32, bf16 = jnp.float32, jnp.bfloat16


def kernel(
    t_ref, q_ref, c_ref, sun_ref, lit_ref, own_ref, tab_ref, cond_ref, planck_ref, insol_ref,
    adv_ref, hum_ref, slot_ref,
    hp, cb, ss, ds, th, tabs, pg, qg, tr_a, tr_b, pd_a, pd_b, zacc, bacc, hk, hz, inc, sf,
    xb, Es, Ss, Fs, iv, nsend, nrecv, esend, erecv, ssend, srecv,
    halo_out, halo_in, slot_out, slot_in,
):
    gx, gy = lax.axis_index("gx"), lax.axis_index("gy")
    barrier = pltpu.get_barrier_semaphore()
    mates = [{"gx": lax.rem(gx + d, N_GX), "gy": gy} for d in range(1, N_GX)]
    beside = [{"gx": gx, "gy": lax.rem(gy + d, N_GY)} for d in (1, N_GY - 1)]
    for one_device in mates + beside:
        pl.semaphore_signal(barrier, inc=1, device_id=one_device, device_id_type=pl.DeviceIdType.MESH)

    trs, pds = (tr_a, tr_b), (pd_a, pd_b)

    eye = lax.broadcasted_iota(jnp.int32, (GP, G), 0) == lax.broadcasted_iota(jnp.int32, (GP, G), 1)

    def column(ref):
        return jnp.sum(jnp.where(eye, ref[...], 0.0), axis=1, keepdims=True)

    ccol = column(cond_ref) * SCALE
    psum, qsum = jnp.sum(planck_ref[...]), jnp.sum(insol_ref[...])
    pg[...] = jnp.broadcast_to(column(planck_ref), (GP, X)).astype(bf16)
    qg[...] = jnp.broadcast_to(column(insol_ref), (GP, X))
    lane16 = lax.broadcasted_iota(jnp.int32, (GP, 16), 1)
    chi = ccol.astype(bf16).astype(f32)
    cext = jnp.where(lane16 == 0, chi, jnp.where(lane16 == 1, ccol - chi, 0.0)).astype(bf16)
    lane = lax.broadcasted_iota(jnp.int32, (R, X), 1)
    line = lax.broadcasted_iota(jnp.int32, (R, X), 0)
    nsend[...] = jnp.zeros_like(nsend)
    ds[0] = jnp.zeros((R, X), f32)

    none = jnp.zeros((R, X), f32)

    def prepare(l, edges):
        tabs[l, :, 0:NT * NQ] = jnp.concatenate(
            [tab_ref[l].astype(f32) * SCALE, jnp.zeros((GP - G, NT * NQ), f32)], axis=0
        ).astype(bf16)
        tabs[l, :, NT * NQ:KW] = cext
        warm, wet = t_ref[l], q_ref[l]
        t = warm.astype(bf16).astype(f32)
        tp = jnp.clip((t + 3.0) * ((NT - 1.0) / 6.0), 0.0, NT - 1.0)
        node = jnp.floor(tp)
        f = tp - node
        below, above = 1.0 - f, none
        for i in range(NT):
            at = node == float(i)
            th[l, i] = jnp.where(at, below, above)
            above = jnp.where(at, f, none)
        s = 1.0 + 0.25 * t
        ss[l] = s
        ds[l] = edges[4] - s
        hp[l] = jnp.clip(wet.astype(bf16).astype(f32) * (NQ - 1.0), 0.0, NQ - 1.0)
        cb[l] = c_ref[l].astype(bf16).astype(f32)
        here = lane == l
        out = []
        for field, v in enumerate((warm, wet)):
            nsend[0, field, pl.ds(l, 1), :] = v[0:1]
            nsend[1, field, pl.ds(l, 1), :] = v[R - 1:R]
            out.append(jnp.where(here, pltpu.roll(v, l, 1), edges[2 * field]))
            out.append(jnp.where(here, pltpu.roll(v, l + 1, 1), edges[2 * field + 1]))
        return tuple(out) + (s,)

    edges = lax.fori_loop(0, L, prepare, (none,) * 5)
    ds[L] = none
    for field in range(2):
        for side in range(2):
            esend[side, field] = edges[2 * field + side]

    i8 = lax.broadcasted_iota(jnp.int32, (NQ, W2), 0).astype(f32)
    ex = (lax.broadcasted_iota(jnp.int32, (16, W2), 0) < 2).astype(f32)
    lr = lax.broadcasted_iota(jnp.int32, (32, 16 * L), 0)
    lc = lax.broadcasted_iota(jnp.int32, (32, 16 * L), 1) >> 4
    selz = jnp.where(
        lr == L, (lc == L - 1).astype(f32), (lc == lr - 1).astype(f32) - (lc == lr).astype(f32)
    ).astype(bf16)
    selb = jnp.where(lr < L, (lc == lr + 1).astype(f32) - (lc == lr).astype(f32), 0.0).astype(bf16)

    def tree(v):
        parts = [v[16 * i:16 * i + 16] for i in range(NC)]
        while len(parts) > 1:
            parts = [a + b for a, b in zip(parts[0::2], parts[1::2])] + (
                [parts[-1]] if len(parts) % 2 else []
            )
        return parts[0]

    def row(ref, r0, *at):
        return jnp.concatenate(
            [ref[(*at, pl.ds(r0, 1), slice(None))], ref[(*at, pl.ds(r0 + 1, 1), slice(None))]], axis=1
        )

    def both(v):
        return jnp.concatenate([v, v], axis=1)

    def depth(p, l, j):
        r0 = 2 * p
        hh = jnp.maximum(0.0, 1.0 - jnp.abs(row(hp, r0, l) - i8))
        w = [row(th, r0, l, i) * hh for i in range(NT)]
        w = [jnp.concatenate(w[2 * i:2 * i + 2], axis=0).astype(bf16) for i in range(NT // 2)]
        w.append((ex * row(cb, r0, l)).astype(bf16))
        xb[j] = jnp.dot(
            tabs[l], jnp.concatenate(w, axis=0), preferred_element_type=f32
        ).astype(bf16)

    def start(p):
        r0 = 2 * p
        sun = row(sun_ref, r0)
        lit = jnp.concatenate(
            [jnp.full((1, X), lit_ref[0, r0 + k].astype(f32)) for k in range(2)], axis=1
        )
        iv[...] = jnp.broadcast_to(
            (1.0 / diffusivity) / sun.astype(bf16).astype(f32), (16, W2)
        ).astype(bf16)
        light = (sun * lit).astype(bf16).astype(f32)
        for k in range(2):
            inc[pl.ds(r0 + k, 1), :] = light[:, X * k:X * k + X]
        Es[...] = both(pg[...]) * row(ds, r0, 0).astype(bf16)
        Ss[...] = (both(qg[...]) * light).astype(bf16)

    def down(p, k, par):
        r0 = 2 * p
        E, S = Es[...], Ss[...]
        inv = jnp.concatenate([iv[...]] * NC, axis=0)
        for j in range(CH):
            l = k * CH + j
            x = xb[j]
            trl = jnp.exp2(x)
            trs[par][l] = trl
            down_part = trl * E
            S = S * jnp.exp2(x * inv)
            zacc[l] = tree(down_part + S)
            step = both(pg[...]) * row(ds, r0, l + 1).astype(bf16)
            pds[par][l + 1] = step
            E = down_part + step
        Es[...] = E
        Ss[...] = S

    def up(k, par):
        F = Fs[...]
        for j in range(CH):
            l = L - 1 - (k * CH + j)
            up_part = trs[par][l] * F
            bacc[l] = tree(up_part)
            F = up_part - pds[par][l]
        Fs[...] = F

    def down_sums(p):
        h = jnp.dot(selz, zacc[...].reshape(16 * L, W2), preferred_element_type=f32)
        hz[...] = h
        for k in range(2):
            sf[pl.ds(2 * p + k, 1), :] = h[L:L + 1, X * k:X * k + X]

    def up_sums(p):
        h = hz[...] + jnp.dot(selb, bacc[...].reshape(16 * L, W2), preferred_element_type=f32)
        for k in range(2):
            hk[pl.ds(2 * p + k, 32, stride=32), :] = h[:, X * k:X * k + X]

    def chunks(body):
        def step(k, carry):
            body(k)
            return carry

        lax.fori_loop(0, NK, step, 0)

    def next_and_down(p, k, par):
        n = p * NK + k + 1
        pn, kn = lax.rem(lax.div(n, NK), PAIRS), lax.rem(n, NK)
        down(p, k, par)
        for j in range(CH):
            depth(pn, kn * CH + j, j)

    def whole(p, par):
        start(p)
        Fs[...] = jnp.zeros((GP, W2), bf16)

        def body(k):
            up(k, 1 - par)
            next_and_down(p, k, par)

        chunks(body)
        up_sums(p - 1)
        down_sums(p)

    for ref in pds:
        ref[0] = jnp.zeros((GP, W2), bf16)
    for j in range(CH):
        depth(0, j, j)
    start(0)
    chunks(lambda k: next_and_down(0, k, 0))
    down_sums(0)

    pl.semaphore_wait(barrier, N_GX + 1)
    west, east = {"gx": lax.rem(gx + N_GX - 1, N_GX), "gy": gy}, {"gx": lax.rem(gx + 1, N_GX), "gy": gy}
    south, north = {"gx": gx, "gy": lax.rem(gy + N_GY - 1, N_GY)}, {"gx": gx, "gy": lax.rem(gy + 1, N_GY)}
    halos = []
    for n, (src, dst, target) in enumerate((
        (esend.at[0], erecv.at[1], west), (esend.at[1], erecv.at[0], east),
        (nsend.at[0], nrecv.at[1], south), (nsend.at[1], nrecv.at[0], north),
    )):
        halos.append(pltpu.make_async_remote_copy(
            src_ref=src, dst_ref=dst, send_sem=halo_out.at[n], recv_sem=halo_in.at[n],
            device_id=target, device_id_type=pl.DeviceIdType.MESH,
        ))
        halos[-1].start()

    def two(i, carry):
        whole(2 * i + 1, 1)
        whole(2 * i + 2, 0)
        return carry

    lax.fori_loop(0, (PAIRS - 2) // 2, two, 0)
    whole(PAIRS - 1, 1)

    surface = (sf[...] + psum * ss[L - 1]) * (1.0 / G)
    own_row = own_ref[...].astype(f32)
    er = lax.broadcasted_iota(jnp.int32, (R, R), 0)
    ec = lax.broadcasted_iota(jnp.int32, (R, R), 1)
    own = jnp.sum(jnp.where(er == ec, own_row, 0.0), axis=1, keepdims=True)
    rank = jnp.sum(
        jnp.where(jnp.logical_and(er < ec, own == own_row), 1.0, 0.0), axis=0, keepdims=True
    )
    pick = lax.broadcasted_iota(jnp.int32, (8 * N_GX, R), 0).astype(f32) == own_row * 8.0 + rank
    slots = jnp.dot(
        pick.astype(f32), surface, precision=lax.Precision.HIGHEST, preferred_element_type=f32
    )
    ssend[...] = slots.reshape(N_GX, 8, X)
    sends = []
    for d in range(1, N_GX):
        to = lax.rem(gx + d, N_GX)
        sends.append(pltpu.make_async_remote_copy(
            src_ref=ssend.at[to], dst_ref=srecv.at[gx], send_sem=slot_out.at[d],
            recv_sem=slot_in.at[d], device_id={"gx": to, "gy": gy},
            device_id_type=pl.DeviceIdType.MESH,
        ))
        sends[-1].start()

    Fs[...] = jnp.zeros((GP, W2), bf16)
    chunks(lambda k: up(k, 1))
    up_sums(PAIRS - 1)

    hk[0:R] = hk[0:R] + qsum * inc[...]
    for copy in halos:
        copy.wait()
    inside_w = (gx > 0).astype(f32)
    inside_e = (gx < N_GX - 1).astype(f32)
    inside_s = (gy > 0).astype(f32)
    inside_n = (gy < N_GY - 1).astype(f32)

    def smooth(l, field, v):
        low = jnp.where(line == 0, nrecv[0, field, pl.ds(l, 1), :] * inside_s, pltpu.roll(v, 1, 0))
        high = jnp.where(
            line == R - 1, nrecv[1, field, pl.ds(l, 1), :] * inside_n, pltpu.roll(v, R - 1, 0)
        )
        left = jnp.where(
            lane == 0, pltpu.roll(erecv[0, field], lax.rem(X - l, X), 1) * inside_w, pltpu.roll(v, 1, 1)
        )
        right = jnp.where(
            lane == X - 1, pltpu.roll(erecv[1, field], X - 1 - l, 1) * inside_e,
            pltpu.roll(v, X - 1, 1),
        )
        return v + diffusion * (low + high + left + right - 4.0 * v)

    def last(i, carry):
        for j in range(5):
            l = 5 * i + j
            gain = hk[pl.ds(pl.multiple_of(R * l, R), R), :] + psum * (ds[l] - ds[l + 1])
            adv_ref[l] = smooth(l, 0, t_ref[l]) + gain * (2.0 / G)
            hum_ref[l] = smooth(l, 1, q_ref[l])
        return carry

    lax.fori_loop(0, L // 5, last, 0)
    for copy in sends:
        copy.wait()
    srecv[gx] = ssend[gx]
    slot_ref[...] = srecv[:, 0:CAP, :]


def hand_over(adv_in, hum_in, slot_in, adv_ref, hum_ref, slot_ref, adv_at, hum_at, slot_at, arrive, leave):
    step = L // 3
    parts = [(slot_in, slot_at, slot_ref)]
    for n in range(3):
        at = pl.ds(n * step, step)
        parts.append((adv_in.at[at], adv_at.at[at], adv_ref.at[at]))
        parts.append((hum_in.at[at], hum_at.at[at], hum_ref.at[at]))
    coming = [pltpu.make_async_copy(a, b, arrive.at[n]) for n, (a, b, _) in enumerate(parts)]
    going = [pltpu.make_async_copy(b, c, leave.at[n]) for n, (_, b, c) in enumerate(parts)]
    for copy in coming:
        copy.start()
    for one, two in zip(coming, going):
        one.wait()
        two.start()
    for copy in going:
        copy.wait()


def on_device(t, q, c, sun, lit, owner, table, cond, planck, insol):
    vmem, scratch = pl.BlockSpec(memory_space=pltpu.VMEM), pltpu.VMEM
    field = scratch((L, R, X), f32)
    levels = scratch((L, GP, W2), bf16)
    state = scratch((GP, W2), bf16)
    out = pl.pallas_call(
        kernel,
        out_shape=(
            jax.ShapeDtypeStruct((L, R, X), f32),
            jax.ShapeDtypeStruct((L, R, X), f32),
            jax.ShapeDtypeStruct((N_GX, CAP, X), f32),
        ),
        in_specs=[vmem] * 4 + [pl.BlockSpec(memory_space=pltpu.SMEM)] + [vmem] * 5,
        out_specs=(vmem,) * 3,
        scratch_shapes=[
            field, field, field, scratch((L + 1, R, X), f32), scratch((L, NT, R, X), f32),
            scratch((L, GP, KW), bf16), scratch((GP, X), bf16), scratch((GP, X), f32),
            levels, levels, scratch((L + 1, GP, W2), bf16), scratch((L + 1, GP, W2), bf16),
            scratch((L, 16, W2), bf16), scratch((L, 16, W2), bf16),
            scratch((32 * R, X), f32), scratch((32, W2), f32), scratch((R, X), f32),
            scratch((R, X), f32), scratch((CH, GP, W2), bf16), state, state, state,
            scratch((16, W2), bf16),
            scratch((2, 2, R, X), f32), scratch((2, 2, R, X), f32),
            scratch((2, 2, R, X), f32), scratch((2, 2, R, X), f32),
            scratch((N_GX, 8, X), f32), scratch((N_GX, 8, X), f32),
            pltpu.SemaphoreType.DMA((4,)), pltpu.SemaphoreType.DMA((4,)),
            pltpu.SemaphoreType.DMA((N_GX,)), pltpu.SemaphoreType.DMA((N_GX,)),
        ],
        compiler_params=pltpu.CompilerParams(
            collective_id=0, has_side_effects=True, vmem_limit_bytes=56 * 2**20
        ),
    )(t, q, c, sun, lit, owner.reshape(1, R), table, cond[None], planck[None], insol[None])
    anywhere = pl.BlockSpec(memory_space=pl.ANY)
    out = pl.pallas_call(
        hand_over,
        out_shape=tuple(jax.ShapeDtypeStruct(v.shape, f32) for v in out),
        in_specs=[anywhere] * 3,
        out_specs=(anywhere,) * 3,
        scratch_shapes=[
            field, field, scratch((N_GX, CAP, X), f32),
            pltpu.SemaphoreType.DMA((7,)), pltpu.SemaphoreType.DMA((7,)),
        ],
        compiler_params=pltpu.CompilerParams(vmem_limit_bytes=60 * 2**20),
    )(*out)
    return out[0], out[1], out[2][None, None]


def solution(mesh):
    placed = (
        P(None, "gy", "gx"),
        P(None, "gy", "gx"),
        P(None, "gy", "gx"),
        P("gy", "gx"),
        P("gx", "gy"),
        P("gx", "gy", None),
        P(),
        P(),
        P(),
        P(),
    )
    return jax.shard_map(
        on_device,
        mesh=mesh,
        in_specs=placed,
        out_specs=(P(None, "gy", "gx"), P(None, "gy", "gx"), P("gy", "gx", None, None, None)),
        check_vma=False,
    )
```
